512 devices in a mesh: shard: 32 (over x, y, core), slot: 16 (over z).
Axes of the slice: x: 4, y: 4, z: 16, core: 2. Of those that a mesh axis runs over, the one named last changes fastest.
Arguments:
- embeddings: bfloat16 [131072, 768], P(('shard', 'slot')), may hold values from -8 to 8
- cluster_ids: int32 [131072], P(('shard', 'slot')), may hold values from 0 to 63, as said below
- order_keys: int32 [131072], P(('shard', 'slot')), may hold values from 0 to 131071, each once
Outputs:
- max_similarity: float32 [131072], P(('shard', 'slot'))
The draws below stay inside these ranges and needn't reach their ends.
Inputs may be any that keep to these rules, and one draw needn't show every extreme that they name: `cluster_ids`: the owner of cluster c is c // 2. Among the 256 rows of one device, at most 8 rows belong to one cluster, and in every device's rows some cluster has exactly 8.
All inputs are finite; a program needn't handle non-finite values.
Results may differ from the reference program's by a relative error of at most 0.00059.
Values may be sent and summed in bfloat16 or wider, within the bound.
A program may use at most 64 MiB of HBM per device.

```python
import math
import jax
import jax.numpy as jnp
from jax import lax

D = 768
ROWS_DEV = 256
CL_DEV = 2
CLUSTERS = 64
CAP = 8
ROWS = 131072
N_SHARD = 32
N_SLOT = 16


def cluster_block(key):
    slots = CLUSTERS * CAP
    first, second, third = jax.random.split(key, 3)
    hot = jax.random.randint(first, (), 0, CLUSTERS)
    places = jnp.arange(slots, dtype=jnp.int32)
    score = jax.random.randint(second, (slots,), 1, 65536)
    score = jnp.where(places // CAP == hot, 0, score) * slots + places
    chosen = jnp.argsort(score)[:ROWS_DEV]
    chosen = chosen[jax.random.permutation(third, ROWS_DEV)]
    return (chosen // CAP).astype(jnp.int32)


def cluster_table(key):
    keys = jax.random.split(key, ROWS // ROWS_DEV)
    return jax.vmap(cluster_block)(keys).reshape(ROWS).astype(jnp.int32)


def draw_cluster_ids(key, part):
    return cluster_table(key)


def draw_embeddings(key, part):
    clusters = cluster_table(key)
    key = jax.random.fold_in(key, 7)
    key_cent, key_fam, key_noise, key_mix, key_spread, key_base = jax.random.split(key, 6)
    family_count = max(1, ROWS // (CLUSTERS * 4))
    family = clusters * family_count + jax.random.randint(key_fam, (ROWS,), 0, family_count)
    centre = jax.vmap(lambda c: jax.random.normal(jax.random.fold_in(key_cent, c), (D,)))(clusters)
    shared = jax.vmap(lambda f: jax.random.normal(jax.random.fold_in(key_base, f), (D,)))(family)
    mix = jnp.exp(jax.random.uniform(key_mix, (ROWS, 1), minval=jnp.log(0.2), maxval=0.0))
    spread = jnp.exp(jax.random.uniform(key_spread, (ROWS, 1), minval=jnp.log(0.15), maxval=jnp.log(1.5)))
    noise = jax.random.normal(key_noise, (ROWS, D))
    values = 0.5 * mix * centre + shared + spread * noise
    return jnp.clip(values, -8.0, 8.0).astype(jnp.bfloat16)


def setup_inputs(seed: int = 0) -> dict:
    arg_keys = jax.random.split(jax.random.key(seed), 4)
    embeddings = draw_embeddings(jax.random.fold_in(arg_keys[3], 71), 0)
    cluster_ids = draw_cluster_ids(jax.random.fold_in(arg_keys[3], 71), 0)
    order_keys = jax.random.permutation(arg_keys[2], ROWS).astype(jnp.int32)
    return dict(embeddings=embeddings, cluster_ids=cluster_ids, order_keys=order_keys)


def unit_rows(values):
    wide = values.astype(jnp.float32)
    return (wide * lax.rsqrt(lax.optimization_barrier(jnp.sum(wide * wide, axis=1, keepdims=True)) + 1e-06)).astype(jnp.bfloat16)

def gram(left, right):
    return lax.dot_general(left, right, (((1,), (1,)), ((), ())), preferred_element_type=jnp.float32)

def reference(embeddings, cluster_ids, order_keys):
    unit = unit_rows(embeddings)
    owner = cluster_ids // CL_DEV
    reach = 2 * ROWS_DEV * N_SLOT
    step = math.gcd(reach, 1024)

    def visit(owner_now, best):
        chosen = jnp.argsort((owner != owner_now).astype(jnp.int32), stable=True)[:reach].astype(jnp.int32)
        valid = owner[chosen] == owner_now
        rows = unit[chosen]
        clusters = jnp.where(valid, cluster_ids[chosen], -1)
        ranks = order_keys[chosen]

        def block(items):
            queries, query_cl, query_rank = items
            sims = gram(queries, rows)
            mask = (query_cl[:, None] == clusters[None, :]) & (clusters[None, :] >= 0) & (ranks[None, :] < query_rank[:, None])
            return lax.optimization_barrier(jnp.max(jnp.where(mask, sims, -1.0), axis=1))
        found = lax.map(block, (rows.reshape(reach // step, step, rows.shape[1]), clusters.reshape(reach // step, step), ranks.reshape(reach // step, step))).reshape(reach)
        return best.at[chosen].set(jnp.where(valid, found, best[chosen]))
    return lax.fori_loop(0, N_SHARD, visit, jnp.full((ROWS,), -1.0, jnp.float32))
```

```python
import jax
import jax.numpy as jnp
from jax import lax
from jax.experimental import pallas as pl
from jax.experimental.pallas import tpu as pltpu
from jax.sharding import PartitionSpec as P

MESH = pl.DeviceIdType.MESH
F32, BF16 = jnp.float32, jnp.bfloat16
NX, NY, NZ = 4, 4, 16
CAP = 8
PER = 16
CHUNKS = NY * NZ // PER
LANES = PER * CAP
BLOCKS = NY * NZ
NEVER = 1e9
A1, A0, R0, R1, L0 = range(5)


def iota(shape, axis):
    return lax.broadcasted_iota(jnp.int32, shape, axis)


def kernel(x_ref, ids_ref, keys_ref, out_ref, place, sent, sent_rank, got, got_rank, rows, ranks, keyed, best, part, other,
           final, back, z_send, z_recv, zr_send, zr_recv, x_send, x_recv, xr_send, xr_recv, p_send, p_recv, b_send, b_recv):
    shard, z = lax.axis_index("shard"), lax.axis_index("slot")
    x, y, core = shard // 8, (shard // 2) % 4, shard % 2

    def at(x_, y_, core_, z_):
        return ((x_ * NY + y_) * 2 + core_, z_)

    def home(r):
        return at(x, (y + r // NZ) % NY, core, (z + r % NZ) % NZ)

    def source(r):
        return at(x, (y + NY - r // NZ) % NY, core, (z + NZ - r % NZ) % NZ)

    right, left = (x + 1) % NX, (x + NX - 1) % NX
    twin = at(x, y, 1 - core, z)
    to_right, to_left = at(right, y, core, z), at(left, y, core, z)
    to_cross, from_cross = at(right, y, 1 - core, z), at(left, y, 1 - core, z)

    barrier = pltpu.get_barrier_semaphore()

    def greet(r, carry):
        pl.semaphore_signal(barrier, inc=1, device_id=source(r), device_id_type=MESH)
        return carry

    lax.fori_loop(1, BLOCKS, greet, 0)
    for device in (twin, to_right, to_left, from_cross):
        pl.semaphore_signal(barrier, inc=1, device_id=device, device_id_type=MESH)

    ids = ids_ref[...]
    idf = ids.astype(F32)
    across = jnp.broadcast_to(idf, (256, 256))
    down = jnp.transpose(across)
    before = (across == down) & (iota((256, 256), 0) < iota((256, 256), 1))
    position = jnp.sum(jnp.where(before, 1.0, 0.0), axis=0, keepdims=True).astype(jnp.int32)
    step_y, step_z = ((ids & 3) + NY - y) & (NY - 1), ((ids >> 2) + NZ - z) & (NZ - 1)
    target = (step_y * NZ + step_z) * CAP + position
    place[...] = jnp.where(iota((BLOCKS * CAP, 256), 0) == target, 1.0, 0.0).astype(BF16)

    wide = x_ref[...].astype(F32)
    unit = (wide * lax.rsqrt(jnp.sum(wide * wide, axis=1, keepdims=True) + 1e-6)).astype(BF16)
    for g in range(CHUNKS):
        laid = jnp.dot(place[g * LANES:(g + 1) * LANES, :], unit, preferred_element_type=F32)
        low = laid[:, :384].reshape(PER, CAP, 384)
        high = laid[:, 384:].reshape(PER, CAP, 384)
        sent[g * PER:(g + 1) * PER] = jnp.concatenate([low, high], axis=1).astype(BF16)

    value = keys_ref[...] + 1
    upper = (value + 256) >> 9
    lower = value - upper * 512
    digits = jnp.where(iota((16, 256), 0) == 0, upper, jnp.where(iota((16, 256), 0) == 1, lower, 0))
    found = lax.dot_general(digits.astype(F32).astype(BF16), place[...], (((1,), (1,)), ((), ())), preferred_element_type=F32)
    value = found[0:1] * 512.0 + found[1:2]
    for g in range(CHUNKS):
        sent_rank[g] = value[:, g * LANES:(g + 1) * LANES]

    pl.semaphore_wait(barrier, BLOCKS - 1 + 4)

    def scatter(r, carry):
        g = r // PER
        pltpu.make_async_remote_copy(src_ref=sent_rank.at[g], dst_ref=got_rank.at[r], send_sem=zr_send, recv_sem=zr_recv.at[g],
                                     device_id=home(r), device_id_type=MESH).start()
        pltpu.make_async_remote_copy(src_ref=sent.at[r], dst_ref=got.at[r], send_sem=z_send, recv_sem=z_recv.at[g],
                                     device_id=home(r), device_id_type=MESH).start()
        return carry

    lax.fori_loop(1, BLOCKS, scatter, 0)
    got[0] = sent[0]
    got_rank[0] = sent_rank[0]
    best[...] = jnp.full(best.shape, -1.0, F32)

    mine = iota((PER, LANES), 1) // CAP == iota((PER, LANES), 0)

    def pass_on(g, a, b, device):
        sends = []
        for i, (ref, send, recv) in enumerate(((rows, x_send, x_recv), (ranks, xr_send, xr_recv))):
            copy = pltpu.make_async_remote_copy(src_ref=ref.at[g, a], dst_ref=ref.at[g, b], send_sem=send.at[g, b], recv_sem=recv.at[g, b],
                                                device_id=device, device_id_type=MESH)
            copy.start()
            sends.append(copy)
        return sends

    def key_side(g, a):
        rank = ranks[g, a]
        rank = jnp.where(rank > 0.5, rank, NEVER)
        keyed[g, a] = jnp.transpose(jnp.broadcast_to(rank, (LANES, LANES)))

    def fold(sims, g, a, h, q):
        masked = jnp.where(keyed[g, a] < ranks[h, q], sims, -1.0)
        best[h, q] = jnp.maximum(best[h, q], jnp.max(masked.reshape(LANES // 8, 8, LANES), axis=0))

    def dots(k, q):
        return lax.dot_general(k, q, (((1,), (1,)), ((), ())), preferred_element_type=F32)

    def inner(g, h):
        sims = dots(rows[g, A0:R1].reshape(2 * LANES, 768), rows[h, A1:R0].reshape(2 * LANES, 768))
        for i, a in enumerate((A0, R0)):
            for j, q in enumerate((A1, A0)):
                fold(sims[i * LANES:(i + 1) * LANES, j * LANES:(j + 1) * LANES], g, a, h, q)

    def outer(g, h):
        sims = dots(rows[g, L0], rows[h, A1:L0].reshape(4 * LANES, 768))
        for j, q in enumerate((A1, A0, R0, R1)):
            fold(sims[:, j * LANES:(j + 1) * LANES], g, L0, h, q)

    def pairs(g, work):
        def one(h, carry):
            work(h, g)
            work(g, h)
            return carry

        lax.fori_loop(0, g, one, 0)
        work(g, g)

    copies = []
    for g in range(CHUNKS):
        first = 1 if g == 0 else 0
        blocks = got.at[pl.ds(g * PER + first, PER - first)]
        pltpu.make_async_copy(blocks, blocks, z_recv.at[g]).wait()
        lanes = got_rank.at[pl.ds(g * PER + first, PER - first)]
        pltpu.make_async_copy(lanes, lanes, zr_recv.at[g]).wait()
        block = got[g * PER:(g + 1) * PER].astype(F32)
        rows[g, A0] = jnp.concatenate([block[:, :CAP].reshape(LANES, 384), block[:, CAP:].reshape(LANES, 384)], axis=1).astype(BF16)
        lane = got_rank[g * PER:(g + 1) * PER].reshape(PER, LANES)
        ranks[g, A0] = jnp.sum(jnp.where(mine, lane, 0.0), axis=0, keepdims=True)
        to_l, to_r, to_t = pass_on(g, A0, R0, to_left), pass_on(g, A0, L0, to_right), pass_on(g, A0, A1, twin)
        key_side(g, A0)
        for copy in to_l:
            copy.wait_recv()
        to_t2 = pass_on(g, R0, R1, twin)
        key_side(g, R0)
        for copy in to_t:
            copy.wait_recv()
        pairs(g, inner)
        for copy in to_r:
            copy.wait_recv()
        key_side(g, L0)
        for copy in to_t2:
            copy.wait_recv()
        pairs(g, outer)
        copies += to_l + to_r + to_t + to_t2

    for g in range(CHUNKS):
        for q in range(4):
            part[q, g] = jnp.max(best[g, q], axis=0, keepdims=True)
    shares = [
        pltpu.make_async_remote_copy(src_ref=part.at[q], dst_ref=other.at[i], send_sem=p_send.at[i], recv_sem=p_recv.at[i],
                                     device_id=device, device_id_type=MESH)
        for i, (q, device) in enumerate(((A1, twin), (R0, to_right), (R1, to_cross)))
    ]
    for copy in shares:
        copy.start()
    for copy in shares:
        copy.wait_recv()
    final[...] = jnp.maximum(jnp.maximum(part[A0], other[0]), jnp.maximum(other[1], other[2]))

    def give(r, carry):
        pltpu.make_async_remote_copy(src_ref=final.at[r // PER], dst_ref=back.at[r], send_sem=b_send, recv_sem=b_recv,
                                     device_id=source(r), device_id_type=MESH).start()
        return carry

    lax.fori_loop(1, BLOCKS, give, 0)
    back[0] = final[0]
    for copy in copies + shares:
        copy.wait_send()
    blocks = sent.at[pl.ds(1, BLOCKS - 1)]
    pltpu.make_async_copy(blocks, blocks, z_send).wait()
    lanes = got_rank.at[pl.ds(1, BLOCKS - 1)]
    pltpu.make_async_copy(lanes, lanes, zr_send).wait()
    lanes = back.at[pl.ds(1, BLOCKS - 1)]
    pltpu.make_async_copy(lanes, lanes, b_recv).wait()
    total = jnp.zeros((1, 256), F32)
    for g in range(CHUNKS):
        lane = back[g * PER:(g + 1) * PER].reshape(PER, LANES)
        held = jnp.sum(jnp.where(mine, lane, 0.0), axis=0, keepdims=True)
        one = held.astype(BF16).astype(F32)
        two = (held - one).astype(BF16).astype(F32)
        three = held - one - two
        row = iota((16, LANES), 0)
        split = jnp.where(row == 0, one, jnp.where(row == 1, two, jnp.where(row == 2, three, 0.0))).astype(BF16)
        picked = jnp.dot(split, place[g * LANES:(g + 1) * LANES, :], preferred_element_type=F32)
        total = total + (picked[0:1] + picked[1:2] + picked[2:3])
    out_ref[...] = total
    pltpu.make_async_copy(lanes, lanes, b_send).wait()


def local(embeddings, cluster_ids, order_keys):
    dma = pltpu.SemaphoreType.DMA
    vmem = pl.BlockSpec(memory_space=pltpu.VMEM)
    out = pl.pallas_call(
        kernel,
        out_shape=jax.ShapeDtypeStruct((1, 256), F32),
        in_specs=[vmem, vmem, vmem],
        out_specs=vmem,
        scratch_shapes=[
            pltpu.VMEM((BLOCKS * CAP, 256), BF16),
            pltpu.VMEM((BLOCKS, 16, 384), BF16),
            pltpu.VMEM((CHUNKS, 1, LANES), F32),
            pltpu.VMEM((BLOCKS, 16, 384), BF16),
            pltpu.VMEM((BLOCKS, 1, LANES), F32),
            pltpu.VMEM((CHUNKS, 5, LANES, 768), BF16),
            pltpu.VMEM((CHUNKS, 5, 1, LANES), F32),
            pltpu.VMEM((CHUNKS, 5, LANES, LANES), F32),
            pltpu.VMEM((CHUNKS, 4, 8, LANES), F32),
            pltpu.VMEM((4, CHUNKS, 1, LANES), F32),
            pltpu.VMEM((3, CHUNKS, 1, LANES), F32),
            pltpu.VMEM((CHUNKS, 1, LANES), F32),
            pltpu.VMEM((BLOCKS, 1, LANES), F32),
            dma, dma((CHUNKS,)), dma, dma((CHUNKS,)),
            dma((CHUNKS, 5)), dma((CHUNKS, 5)), dma((CHUNKS, 5)), dma((CHUNKS, 5)),
            dma((3,)), dma((3,)), dma, dma,
        ],
        compiler_params=pltpu.CompilerParams(collective_id=0, has_side_effects=True, vmem_limit_bytes=40 * 2**20),
    )(embeddings, cluster_ids.reshape(1, 256), order_keys.reshape(1, 256))
    return out.reshape(256)


def solution(mesh):
    placed = (P(("shard", "slot"), None), P(("shard", "slot")), P(("shard", "slot")))
    return jax.shard_map(local, mesh=mesh, in_specs=placed, out_specs=P(("shard", "slot")), check_vma=False)
```

```python
import jax
import jax.numpy as jnp
from jax import lax
from jax.experimental import pallas as pl
from jax.experimental.pallas import tpu as pltpu
from jax.sharding import PartitionSpec as P

MESH = pl.DeviceIdType.MESH
F32, BF16 = jnp.float32, jnp.bfloat16
NX, NY, NZ = 4, 4, 16
D, CAP = 768, 8
ROWS = 256
BIG, SMALL = 128, 64
SUB = 4
SUBS = NZ // SUB
PLACES = SUB * CAP
LAG = 2
NEVER = 1e9
ORDER = (0, 1, 3, 2)
A1, A0, R0, R1, L0 = range(5)


def iota(shape, axis):
    return lax.broadcasted_iota(jnp.int32, shape, axis)


def way(b):
    return 8 + b // 2 - (b % 2) * (1 + 2 * (b // 2))


def turn(rows):
    group = iota((1, 128), 1) // 32
    out = []
    for j in range(4):
        row = rows[0] if j == 0 else pltpu.roll(rows[0], (32 * (0 - j)) % 128, 1)
        for i in range(1, 4):
            shift = (32 * (i - j)) % 128
            row = jnp.where(group == i, rows[i] if shift == 0 else pltpu.roll(rows[i], shift, 1), row)
        out.append(row)
    return out


def collect(ref):
    held = ref[...].reshape(NZ, 128)
    held = jnp.where((iota((NZ, 128), 1) // CAP) % 4 == iota((NZ, 128), 0) % 4, held, 0.0)
    return turn([jnp.sum(held[4 * q:4 * q + 4], axis=0, keepdims=True) for q in range(4)])


def kernel(x_hbm, ids_hbm, keys_hbm, out_ref, x_ref, ids_ref, keys_ref, place, sent, stage, got, rank_out, rank_mid,
           rank_turned, rank_got, ranks, big, small, keyed, query, best, part, half, whole, other, turned, back,
           in_sem, y_send, y_recv, yr_send, yr_recv, z_send, z_recv, zr_send, zr_recv, x_send, x_recv, xr_send, xr_recv,
           h_send, h_recv, p_send, p_recv, b_send, b_recv):
    shard, z = lax.axis_index("shard"), lax.axis_index("slot")
    x, y, core = shard // 8, (shard // 2) % 4, shard % 2

    def at(dx, dy, flip, dz):
        core_ = 1 - core if flip else core
        return ((((x + dx) % NX) * NY + (y + dy) % NY) * 2 + core_, (z + dz) % NZ)

    twin, right, left = at(0, 0, True, 0), at(1, 0, False, 0), at(3, 0, False, 0)

    def remote(src, dst, send, recv, device):
        return pltpu.make_async_remote_copy(src_ref=src, dst_ref=dst, send_sem=send, recv_sem=recv, device_id=device,
                                            device_id_type=MESH)

    def await_bytes(ref, sem):
        pltpu.make_async_copy(ref, ref, sem).wait()

    loads = [pltpu.make_async_copy(a, b, in_sem.at[i])
             for i, (a, b) in enumerate(((ids_hbm, ids_ref), (keys_hbm, keys_ref), (x_hbm, x_ref)))]
    for load in loads:
        load.start()

    barrier = pltpu.get_barrier_semaphore()

    def greet(device):
        pl.semaphore_signal(barrier, inc=1, device_id=device, device_id_type=MESH)

    def greet_z(d, carry):
        greet(at(0, 0, False, d))
        return carry

    for device in (twin, right):
        greet(device)
    for g in range(NY):
        greet(at(3, g, False, 0))
        if g:
            greet(at(0, g, False, 0))
    lax.fori_loop(1, NZ, greet_z, 0)

    loads[0].wait()
    ids = ids_ref[...]
    across = jnp.broadcast_to(ids.astype(F32), (ROWS, ROWS))
    before = (across == jnp.transpose(across)) & (iota((ROWS, ROWS), 0) < iota((ROWS, ROWS), 1))
    position = jnp.sum(jnp.where(before, 1.0, 0.0), axis=0, keepdims=True).astype(jnp.int32)
    step_y, step_z = ((ids & 3) + NY - y) & (NY - 1), ((ids >> 2) + NZ - z) & (NZ - 1)
    block = jnp.where(step_z < 8, 15 - 2 * step_z, 2 * step_z - 16)
    target = (step_y * NZ + block) * CAP + position
    place[...] = jnp.where(iota((NY * BIG, ROWS), 0) == target, 1.0, 0.0).astype(BF16)

    loads[1].wait()
    value = keys_ref[...] + 1
    upper = (value + 256) >> 9
    lower = value - upper * 512
    digits = jnp.where(iota((16, ROWS), 0) == 0, upper, jnp.where(iota((16, ROWS), 0) == 1, lower, 0))
    found = lax.dot_general(digits.astype(F32).astype(BF16), place[...], (((1,), (1,)), ((), ())), preferred_element_type=F32)
    value = found[0:1] * 512.0 + found[1:2]
    for g in range(NY):
        rank_out[g] = value[:, g * BIG:(g + 1) * BIG]

    loads[2].wait()
    wide = x_ref[...].astype(F32)
    unit = (wide * lax.rsqrt(jnp.sum(wide * wide, axis=1, keepdims=True) + 1e-6)).astype(BF16)
    for g in range(NY):
        laid = jnp.dot(place[g * BIG:(g + 1) * BIG, :], unit, preferred_element_type=F32)
        halves = [laid[:, :D // 2].reshape(NZ, CAP, D // 2), laid[:, D // 2:].reshape(NZ, CAP, D // 2)]
        sent[g] = jnp.concatenate(halves, axis=1).astype(BF16)

    pl.semaphore_wait(barrier, 24)

    def along_z(g, source):
        def go(b, carry):
            remote(source.at[g, b], got.at[g, b], z_send, z_recv.at[g, b // SUB], at(0, 0, False, way(b))).start()
            return carry

        lax.fori_loop(0, NZ - 1, go, 0)
        got[g, NZ - 1] = source[g, NZ - 1]

    for g in ORDER[1:]:
        remote(rank_out.at[g], rank_mid.at[g], yr_send, yr_recv, at(0, g, False, 0)).start()
    along_y = {g: remote(sent.at[g], stage.at[g], y_send.at[g], y_recv.at[g], at(0, g, False, 0)) for g in ORDER[1:]}
    along_y[1].start()
    along_z(0, sent)
    along_y[3].start()
    along_y[2].start()

    best[...] = jnp.full(best.shape, -1.0, F32)
    await_bytes(rank_mid.at[pl.ds(1, NY - 1)], yr_recv)
    for q, row in enumerate(turn([rank_out[0]] + [rank_mid[g] for g in range(1, NY)])):
        rank_turned[q] = row

    def ranks_along_z(b, carry):
        remote(rank_turned.at[b // SUB], rank_got.at[b], zr_send, zr_recv, at(0, 0, False, way(b))).start()
        return carry

    lax.fori_loop(0, NZ - 1, ranks_along_z, 0)
    rank_got[NZ - 1] = rank_turned[SUBS - 1]
    for g in ORDER[1:]:
        along_y[g].wait_recv()
        along_z(g, stage)

    await_bytes(rank_got.at[pl.ds(0, NZ - 1)], zr_recv)
    for g, row in enumerate(collect(rank_got)):
        ranks[A0, g] = row
    shared = [remote(ranks.at[a], ranks.at[b], xr_send.at[i], xr_recv.at[i], device)
              for i, (a, b, device) in enumerate(((A0, R0, left), (A0, L0, right), (A0, A1, twin), (R0, R1, twin)))]
    for copy in shared[:3]:
        copy.start()

    def rows_of(i, sub, a):
        if i < 3:
            return big.at[i, a, pl.ds(sub * PLACES, PLACES)]
        return small.at[sub // 2, a, pl.ds(sub % 2 * PLACES, PLACES)]

    def passed(i, sub, j):
        a, b, device = ((A0, R0, left), (A0, L0, right), (A0, A1, twin), (R0, R1, twin))[j]
        return remote(rows_of(i, sub, a), rows_of(i, sub, b), x_send.at[j], x_recv.at[i * SUBS + sub, j], device)

    def pass_on(i, sub):
        g = ORDER[i]
        first = sub * SUB
        count = SUB - 1 if sub == SUBS - 1 else SUB
        await_bytes(got.at[g, pl.ds(first, count)], z_recv.at[g, sub])
        held = got[g, first:first + SUB].astype(F32)
        rows = jnp.concatenate([held[:, :CAP].reshape(PLACES, D // 2), held[:, CAP:].reshape(PLACES, D // 2)], axis=1)
        rows_of(i, sub, A0)[...] = rows.astype(BF16)
        for j in range(3):
            passed(i, sub, j).start()

    def pass_twin(i, sub):
        passed(i, sub, 0).wait_recv()
        passed(i, sub, 3).start()

    def learn_ranks():
        for copy in shared[:3]:
            copy.wait_recv()
        shared[3].start()
        for i, g in enumerate(ORDER):
            for s, a in enumerate((A0, R0, L0)):
                rank = ranks[a, g]
                rank = jnp.where(rank > 0.5, rank, NEVER)
                keyed[i, s] = jnp.transpose(jnp.broadcast_to(rank, (BIG, BIG)))
        shared[3].wait_recv()
        for i in range(3):
            for a in (A1, A0, R0, R1):
                query[4 * i + a] = ranks[a, ORDER[i]]
        low = iota((1, BIG), 1) < SMALL
        for s, (a, b) in enumerate(((A1, A0), (R0, R1))):
            one, two = ranks[a, ORDER[3]], ranks[b, ORDER[3]]
            query[12 + s] = jnp.where(low, one, pltpu.roll(two, SMALL, 1))
            query[14 + s] = jnp.where(low, pltpu.roll(one, SMALL, 1), two)

    def dots(k, q):
        return lax.dot_general(k, q, (((1,), (1,)), ((), ())), preferred_element_type=F32)

    def rows_in(p, a, b):
        if isinstance(p, int) and p >= 3:
            return small[p - 3, a:b].reshape((b - a) * SMALL, D)
        return big[p, a:b].reshape((b - a) * BIG, D)

    def key_ranks(p, s):
        if isinstance(p, int) and p >= 3:
            return keyed[3, s, (p - 3) * SMALL:(p - 2) * SMALL]
        return keyed[p, s]

    def groups(q, outer):
        if isinstance(q, int) and q >= 3:
            return [12 + 2 * (q - 3) + s for s in range(2 if outer else 1)]
        return [4 * q + a for a in range(4 if outer else 2)]

    def fold(sims, rank, j):
        masked = jnp.where(rank < query[j], sims, -1.0)
        best[j] = jnp.maximum(best[j], jnp.max(masked.reshape(sims.shape[0] // 8, 8, 128), axis=0))

    def inner(k, q):
        sims = dots(rows_in(k, A0, R1), rows_in(q, A1, R0))
        size = sims.shape[0] // 2
        for s in range(2):
            for n, j in enumerate(groups(q, False)):
                fold(sims[s * size:(s + 1) * size, n * 128:(n + 1) * 128], key_ranks(k, s), j)

    def outer(k, q):
        sims = dots(rows_in(k, L0, L0 + 1), rows_in(q, A1, L0))
        for n, j in enumerate(groups(q, True)):
            fold(sims[:, n * 128:(n + 1) * 128], key_ranks(k, 2), j)

    def pairs(p, work):
        def one(h, carry):
            work(h, p)
            work(p, h)
            return carry

        lax.fori_loop(0, min(p, 3), one, 0)
        if p == 4:
            work(3, 4)
            work(4, 3)
        work(p, p)

    def subs_of(p):
        return [(p, sub) for sub in range(SUBS)] if p < 3 else [(3, 2 * (p - 3)), (3, 2 * (p - 3) + 1)]

    def compare_inner(p):
        for i, sub in subs_of(p):
            passed(i, sub, 2).wait_recv()
        pairs(p, inner)

    def compare_outer(p):
        for i, sub in subs_of(p):
            passed(i, sub, 1).wait_recv()
            passed(i, sub, 3).wait_recv()
        pairs(p, outer)

    for n in range(4 * SUBS):
        pass_on(n // SUBS, n % SUBS)
        if n == 0:
            learn_ranks()
        if n >= LAG:
            pass_twin((n - LAG) // SUBS, (n - LAG) % SUBS)
        i, sub = divmod(n - LAG, SUBS)
        if sub == SUBS - 1 and 0 <= i < 3:
            compare_inner(i)
        if sub == 0 and 0 < i < 4:
            compare_outer(i - 1)
    compare_inner(3)
    compare_outer(3)
    for n in range(4 * SUBS - LAG, 4 * SUBS):
        pass_twin(n // SUBS, n % SUBS)
    compare_inner(4)
    compare_outer(4)

    low = iota((1, BIG), 1) < SMALL
    top = [jnp.max(best[j], axis=0, keepdims=True) for j in range(16)]
    for a in (A1, A0, R0, R1):
        for i in range(3):
            part[a, ORDER[i]] = top[4 * i + a]
        one, two = top[12 + a // 2], top[14 + a // 2]
        part[a, ORDER[3]] = (jnp.where(low, one, pltpu.roll(two, SMALL, 1)) if a in (A1, R0) else
                             jnp.where(low, pltpu.roll(one, SMALL, 1), two))
    halves = [remote(part.at[a], half.at[i], h_send.at[i], h_recv.at[i], twin) for i, a in enumerate((R1, A1))]
    for copy in halves:
        copy.start()
    for n, (a, dx) in enumerate(((R0, 1), (A0, 0))):
        halves[n].wait_recv()
        for g in (2, 1, 3, 0):
            whole[n, g] = jnp.maximum(part[a, g], half[n, g])
            if dx or g:
                remote(whole.at[n, g], other.at[n, g], p_send, p_recv.at[n], at(dx, NY - g, False, 0)).start()
    other[1, 0] = whole[1, 0]
    await_bytes(other.at[0], p_recv.at[0])
    await_bytes(other.at[1, pl.ds(1, 3)], p_recv.at[1])
    most = [jnp.maximum(other[0, g], other[1, g]) for g in range(NY)]
    for q, row in enumerate(turn(most)):
        turned[q] = row

    def give(b, carry):
        remote(turned.at[b // SUB], back.at[b], b_send, b_recv, at(0, 0, False, NZ - way(b))).start()
        return carry

    lax.fori_loop(0, NZ - 1, give, 0)
    back[NZ - 1] = turned[SUBS - 1]

    for g in ORDER[1:]:
        along_y[g].wait_send()
    for copy in shared:
        copy.wait_send()
    await_bytes(rank_mid.at[pl.ds(1, NY - 1)], yr_send)
    await_bytes(rank_got.at[pl.ds(0, NZ - 1)], zr_send)
    await_bytes(got.at[:, pl.ds(0, NZ - 1)], z_send)
    for j in range(4):
        await_bytes(got, x_send.at[j])
    for copy in halves:
        copy.wait_send()
    await_bytes(back.at[pl.ds(0, 7)], p_send)

    await_bytes(back.at[pl.ds(0, NZ - 1)], b_recv)
    total = jnp.zeros((1, ROWS), F32)
    for g, held in enumerate(collect(back)):
        one = held.astype(BF16).astype(F32)
        two = (held - one).astype(BF16).astype(F32)
        three = held - one - two
        row = iota((16, BIG), 0)
        split = jnp.where(row == 0, one, jnp.where(row == 1, two, jnp.where(row == 2, three, 0.0))).astype(BF16)
        picked = jnp.dot(split, place[g * BIG:(g + 1) * BIG, :], preferred_element_type=F32)
        total = total + (picked[0:1] + picked[1:2] + picked[2:3])
    out_ref[...] = total
    await_bytes(back.at[pl.ds(0, NZ - 1)], b_send)


def local(embeddings, cluster_ids, order_keys):
    dma = pltpu.SemaphoreType.DMA
    vmem = pltpu.VMEM
    out = pl.pallas_call(
        kernel,
        out_shape=jax.ShapeDtypeStruct((1, ROWS), F32),
        in_specs=[pl.BlockSpec(memory_space=pl.ANY)] * 3,
        out_specs=pl.BlockSpec(memory_space=vmem),
        scratch_shapes=[
            vmem((ROWS, D), BF16),
            vmem((1, ROWS), jnp.int32),
            vmem((1, ROWS), jnp.int32),
            vmem((NY * BIG, ROWS), BF16),
            vmem((NY, NZ, 16, D // 2), BF16),
            vmem((NY, NZ, 16, D // 2), BF16),
            vmem((NY, NZ, 16, D // 2), BF16),
            vmem((NY, 1, BIG), F32),
            vmem((NY, 1, BIG), F32),
            vmem((SUBS, 1, BIG), F32),
            vmem((NZ, 1, BIG), F32),
            vmem((5, NY, 1, BIG), F32),
            vmem((3, 5, BIG, D), BF16),
            vmem((2, 5, SMALL, D), BF16),
            vmem((4, 3, BIG, BIG), F32),
            vmem((16, 1, BIG), F32),
            vmem((16, 8, BIG), F32),
            vmem((4, NY, 1, BIG), F32),
            vmem((2, NY, 1, BIG), F32),
            vmem((2, NY, 1, BIG), F32),
            vmem((2, NY, 1, BIG), F32),
            vmem((SUBS, 1, BIG), F32),
            vmem((NZ, 1, BIG), F32),
            dma((3,)), dma((NY,)), dma((NY,)), dma, dma, dma, dma((NY, SUBS)), dma, dma,
            dma((4,)), dma((4 * SUBS, 4)), dma((4,)), dma((4,)), dma((2,)), dma((2,)), dma, dma((2,)), dma, dma,
        ],
        compiler_params=pltpu.CompilerParams(collective_id=0, has_side_effects=True, vmem_limit_bytes=56 * 2**20),
    )(embeddings, cluster_ids.reshape(1, ROWS), order_keys.reshape(1, ROWS))
    return out.reshape(ROWS)


def solution(mesh):
    placed = (P(("shard", "slot"), None), P(("shard", "slot")), P(("shard", "slot")))
    return jax.shard_map(local, mesh=mesh, in_specs=placed, out_specs=P(("shard", "slot")), check_vma=False)
```

```python
import jax
import jax.numpy as jnp
from jax import lax
from jax.experimental import pallas as pl
from jax.experimental.pallas import tpu as pltpu
from jax.sharding import PartitionSpec as P

MESH = pl.DeviceIdType.MESH
F32, BF16 = jnp.float32, jnp.bfloat16
NX, NY, NZ = 4, 4, 16
D, CAP = 768, 8
ROWS = 256
BIG, SMALL = 128, 64
SUB = 4
SUBS = NZ // SUB
PLACES = SUB * CAP
AHEAD = 6
LAG = 2
NEVER = 1e9
ORDER = (0, 1, 3, 2)
A1, A0, R0, R1, L0 = range(5)


def iota(shape, axis):
    return lax.broadcasted_iota(jnp.int32, shape, axis)


WAY = (1, 15, 2, 14, 3, 13, 4, 12, 5, 11, 6, 10, 7, 9, 8, 0)


def turn(rows):
    group = iota((1, 128), 1) // 32
    out = []
    for j in range(4):
        row = rows[0] if j == 0 else pltpu.roll(rows[0], (32 * (0 - j)) % 128, 1)
        for i in range(1, 4):
            shift = (32 * (i - j)) % 128
            row = jnp.where(group == i, rows[i] if shift == 0 else pltpu.roll(rows[i], shift, 1), row)
        out.append(row)
    return out


def collect(ref):
    held = ref[...].reshape(NZ, 128)
    held = jnp.where((iota((NZ, 128), 1) // CAP) % 4 == iota((NZ, 128), 0) % 4, held, 0.0)
    return turn([jnp.sum(held[4 * q:4 * q + 4], axis=0, keepdims=True) for q in range(4)])


def kernel(x_hbm, ids_hbm, keys_hbm, out_ref, x_ref, ids_ref, keys_ref, place, sent, stage, got, rank_out, rank_mid,
           rank_turned, rank_got, ranks, big, small, keyed, query, best, part, half, whole, other, turned, back,
           in_sem, ready, y_send, y_recv, yr_send, yr_recv, z_send, z_recv, zr_send, zr_recv, x_send, x_recv, xr_send, xr_recv,
           h_send, h_recv, p_send, p_recv, b_send, b_recv):
    shard, z = lax.axis_index("shard"), lax.axis_index("slot")
    x, y, core = shard // 8, (shard // 2) % 4, shard % 2

    def at(dx, dy, flip, dz):
        core_ = 1 - core if flip else core
        return ((((x + dx) % NX) * NY + (y + dy) % NY) * 2 + core_, (z + dz) % NZ)

    twin, right, left = at(0, 0, True, 0), at(1, 0, False, 0), at(3, 0, False, 0)

    def remote(src, dst, send, recv, device):
        return pltpu.make_async_remote_copy(src_ref=src, dst_ref=dst, send_sem=send, recv_sem=recv, device_id=device,
                                            device_id_type=MESH)

    def await_bytes(ref, sem):
        pltpu.make_async_copy(ref, ref, sem).wait()

    loads = [pltpu.make_async_copy(a, b, in_sem.at[i])
             for i, (a, b) in enumerate(((ids_hbm, ids_ref), (keys_hbm, keys_ref), (x_hbm, x_ref)))]
    for load in loads:
        load.start()

    barrier = pltpu.get_barrier_semaphore()

    def greet(device):
        pl.semaphore_signal(barrier, inc=1, device_id=device, device_id_type=MESH)

    def greet_z(d, carry):
        greet(at(0, 0, False, d))
        return carry

    above, below = at(0, 0, False, 1), at(0, 0, False, 15)
    for device in (twin, right, left, above, below):
        greet(device)
    for g in range(1, NY):
        greet(at(3, g, False, 0))
        greet(at(0, g, False, 0))

    loads[0].wait()
    ids = ids_ref[...]
    across = jnp.broadcast_to(ids.astype(F32), (ROWS, ROWS))
    before = (across == jnp.transpose(across)) & (iota((ROWS, ROWS), 0) < iota((ROWS, ROWS), 1))
    position = jnp.sum(jnp.where(before, 1.0, 0.0), axis=0, keepdims=True).astype(jnp.int32)
    step_y, step_z = ((ids & 3) + NY - y) & (NY - 1), ((ids >> 2) + NZ - z) & (NZ - 1)
    block = jnp.zeros_like(ids)
    for b in range(NZ):
        block = jnp.where(step_z == WAY[b], b, block)
    target = (step_y * NZ + block) * CAP + position
    place[...] = jnp.where(iota((NY * BIG, ROWS), 0) == target, 1.0, 0.0).astype(BF16)

    loads[1].wait()
    value = keys_ref[...] + 1
    upper = (value + 256) >> 9
    lower = value - upper * 512
    digits = jnp.where(iota((16, ROWS), 0) == 0, upper, jnp.where(iota((16, ROWS), 0) == 1, lower, 0))
    found = lax.dot_general(digits.astype(F32).astype(BF16), place[...], (((1,), (1,)), ((), ())), preferred_element_type=F32)
    value = found[0:1] * 512.0 + found[1:2]
    for g in range(NY):
        rank_out[g] = value[:, g * BIG:(g + 1) * BIG]

    loads[2].wait()
    wide = x_ref[...].astype(F32)
    unit = (wide * lax.rsqrt(jnp.sum(wide * wide, axis=1, keepdims=True) + 1e-6)).astype(BF16)
    for g in range(NY):
        laid = jnp.dot(place[g * BIG:(g + 1) * BIG, :], unit, preferred_element_type=F32)
        halves = [laid[:, :D // 2].reshape(NZ, CAP, D // 2), laid[:, D // 2:].reshape(NZ, CAP, D // 2)]
        sent[g] = jnp.concatenate(halves, axis=1).astype(BF16)

    pl.semaphore_wait(barrier, 11)

    def tell(d):
        pl.semaphore_signal(ready.at[0, d], inc=1, device_id=below, device_id_type=MESH)
        if d < NZ // 2:
            pl.semaphore_signal(ready.at[1, d], inc=1, device_id=above, device_id_type=MESH)

    def hear(d):
        pl.semaphore_wait(ready.at[0, d], 1)
        if d < NZ // 2:
            pl.semaphore_wait(ready.at[1, d], 1)
            tell(d + 1)

    tell(2)

    def along_z(n):
        i, sub = divmod(n, SUBS)
        g, source = ORDER[i], stage if i else sent
        if i and sub == 0:
            along_y[g].wait_recv()
        for b in range(sub * SUB, (sub + 1) * SUB):
            if i == 0 and b % 2 == 0 and b >= 2:
                hear(WAY[b])
            if WAY[b]:
                remote(source.at[g, b], got.at[g, b], z_send, z_recv.at[g, sub], at(0, 0, False, WAY[b])).start()
            else:
                got[g, b] = source[g, b]

    for g in ORDER[1:]:
        remote(rank_out.at[g], rank_mid.at[g], yr_send, yr_recv, at(0, g, False, 0)).start()
    along_y = {g: remote(sent.at[g], stage.at[g], y_send.at[g], y_recv.at[g], at(0, g, False, 0)) for g in ORDER[1:]}
    for g in ORDER[1:]:
        along_y[g].start()
    for n in range(SUBS):
        along_z(n)

    best[...] = jnp.full(best.shape, -1.0, F32)
    await_bytes(rank_mid.at[pl.ds(1, NY - 1)], yr_recv)
    for q, row in enumerate(turn([rank_out[0]] + [rank_mid[g] for g in range(1, NY)])):
        rank_turned[q] = row

    for b in range(NZ - 1):
        remote(rank_turned.at[b // SUB], rank_got.at[b], zr_send, zr_recv, at(0, 0, False, WAY[b])).start()
    rank_got[NZ - 1] = rank_turned[SUBS - 1]
    for n in range(SUBS, AHEAD):
        along_z(n)

    shared = [remote(ranks.at[a], ranks.at[b], xr_send.at[i], xr_recv.at[i], device)
              for i, (a, b, device) in enumerate(((A0, R0, left), (A0, L0, right), (A0, A1, twin), (R0, R1, twin)))]

    def gather_ranks():
        await_bytes(rank_got.at[pl.ds(0, NZ - 1)], zr_recv)
        for g, row in enumerate(collect(rank_got)):
            ranks[A0, g] = row
        for copy in shared[:3]:
            copy.start()

    def rows_of(i, sub, a):
        if i < 3:
            return big.at[i, a, pl.ds(sub * PLACES, PLACES)]
        return small.at[sub // 2, a, pl.ds(sub % 2 * PLACES, PLACES)]

    def passed(i, sub, j):
        a, b, device = ((A0, R0, left), (A0, L0, right), (A0, A1, twin), (R0, R1, twin))[j]
        return remote(rows_of(i, sub, a), rows_of(i, sub, b), x_send.at[j], x_recv.at[i * SUBS + sub, j], device)

    def pass_on(i, sub):
        g = ORDER[i]
        first = sub * SUB
        count = SUB - 1 if sub == SUBS - 1 else SUB
        await_bytes(got.at[g, pl.ds(first, count)], z_recv.at[g, sub])
        held = got[g, first:first + SUB].astype(F32)
        rows = jnp.concatenate([held[:, :CAP].reshape(PLACES, D // 2), held[:, CAP:].reshape(PLACES, D // 2)], axis=1)
        rows_of(i, sub, A0)[...] = rows.astype(BF16)
        for j in range(3):
            passed(i, sub, j).start()

    def pass_twin(i, sub):
        passed(i, sub, 0).wait_recv()
        passed(i, sub, 3).start()

    def learn_ranks():
        for copy in shared[:3]:
            copy.wait_recv()
        shared[3].start()
        for i, g in enumerate(ORDER):
            for s, a in enumerate((A0, R0, L0)):
                rank = ranks[a, g]
                rank = jnp.where(rank > 0.5, rank, NEVER)
                keyed[i, s] = jnp.transpose(jnp.broadcast_to(rank, (BIG, BIG)))
        shared[3].wait_recv()
        for i in range(3):
            for a in (A1, A0, R0, R1):
                query[4 * i + a] = ranks[a, ORDER[i]]
        low = iota((1, BIG), 1) < SMALL
        for s, (a, b) in enumerate(((A1, A0), (R0, R1))):
            one, two = ranks[a, ORDER[3]], ranks[b, ORDER[3]]
            query[12 + s] = jnp.where(low, one, pltpu.roll(two, SMALL, 1))
            query[14 + s] = jnp.where(low, pltpu.roll(one, SMALL, 1), two)

    def dots(k, q):
        return lax.dot_general(k, q, (((1,), (1,)), ((), ())), preferred_element_type=F32)

    def rows_in(p, a, b):
        if isinstance(p, int) and p >= 3:
            return small[p - 3, a:b].reshape((b - a) * SMALL, D)
        return big[p, a:b].reshape((b - a) * BIG, D)

    def key_ranks(p, s):
        if isinstance(p, int) and p >= 3:
            return keyed[3, s, (p - 3) * SMALL:(p - 2) * SMALL]
        return keyed[p, s]

    def groups(q, outer):
        if isinstance(q, int) and q >= 3:
            return [12 + 2 * (q - 3) + s for s in range(2 if outer else 1)]
        return [4 * q + a for a in range(4 if outer else 2)]

    def fold(sims, rank, j):
        masked = jnp.where(rank < query[j], sims, -1.0)
        best[j] = jnp.maximum(best[j], jnp.max(masked.reshape(sims.shape[0] // 8, 8, 128), axis=0))

    def inner(k, q):
        sims = dots(rows_in(k, A0, R1), rows_in(q, A1, R0))
        size = sims.shape[0] // 2
        for s in range(2):
            for n, j in enumerate(groups(q, False)):
                fold(sims[s * size:(s + 1) * size, n * 128:(n + 1) * 128], key_ranks(k, s), j)

    def outer(k, q):
        sims = dots(rows_in(k, L0, L0 + 1), rows_in(q, A1, L0))
        for n, j in enumerate(groups(q, True)):
            fold(sims[:, n * 128:(n + 1) * 128], key_ranks(k, 2), j)

    def pairs(p, work):
        def one(h, carry):
            work(h, p)
            work(p, h)
            return carry

        lax.fori_loop(0, min(p, 3), one, 0)
        if p == 4:
            work(3, 4)
            work(4, 3)
        work(p, p)

    def subs_of(p):
        return [(p, sub) for sub in range(SUBS)] if p < 3 else [(3, 2 * (p - 3)), (3, 2 * (p - 3) + 1)]

    def compare_inner(p):
        for i, sub in subs_of(p):
            passed(i, sub, 2).wait_recv()
        pairs(p, inner)

    def compare_outer(p):
        for i, sub in subs_of(p):
            passed(i, sub, 1).wait_recv()
            passed(i, sub, 3).wait_recv()
        pairs(p, outer)

    for n in range(4 * SUBS):
        pass_on(n // SUBS, n % SUBS)
        if n + AHEAD < 4 * SUBS:
            along_z(n + AHEAD)
        if n == 1:
            gather_ranks()
        if n == SUBS:
            learn_ranks()
        if n >= LAG:
            pass_twin((n - LAG) // SUBS, (n - LAG) % SUBS)
        i, sub = divmod(n - LAG, SUBS)
        if sub == SUBS - 1 and 0 <= i < 3:
            compare_inner(i)
        if sub == 0 and 0 < i < 4:
            compare_outer(i - 1)
    compare_inner(3)
    compare_outer(3)
    for n in range(4 * SUBS - LAG, 4 * SUBS):
        pass_twin(n // SUBS, n % SUBS)
    compare_inner(4)
    compare_outer(4)

    low = iota((1, BIG), 1) < SMALL
    top = [jnp.max(best[j], axis=0, keepdims=True) for j in range(16)]
    for a in (A1, A0, R0, R1):
        for i in range(3):
            part[a, ORDER[i]] = top[4 * i + a]
        one, two = top[12 + a // 2], top[14 + a // 2]
        part[a, ORDER[3]] = (jnp.where(low, one, pltpu.roll(two, SMALL, 1)) if a in (A1, R0) else
                             jnp.where(low, pltpu.roll(one, SMALL, 1), two))
    halves = [remote(part.at[a], half.at[i], h_send.at[i], h_recv.at[i], twin) for i, a in enumerate((R1, A1))]
    for copy in halves:
        copy.start()
    for n, (a, dx) in enumerate(((R0, 1), (A0, 0))):
        halves[n].wait_recv()
        for g in (2, 1, 3, 0):
            whole[n, g] = jnp.maximum(part[a, g], half[n, g])
            if dx or g:
                remote(whole.at[n, g], other.at[n, g], p_send, p_recv.at[n], at(dx, NY - g, False, 0)).start()
    other[1, 0] = whole[1, 0]
    await_bytes(other.at[0], p_recv.at[0])
    await_bytes(other.at[1, pl.ds(1, 3)], p_recv.at[1])
    most = [jnp.maximum(other[0, g], other[1, g]) for g in range(NY)]
    for q, row in enumerate(turn(most)):
        turned[q] = row

    for b in range(NZ - 1):
        remote(turned.at[b // SUB], back.at[b], b_send, b_recv, at(0, 0, False, NZ - WAY[b])).start()
    back[NZ - 1] = turned[SUBS - 1]

    for g in ORDER[1:]:
        along_y[g].wait_send()
    for copy in shared:
        copy.wait_send()
    await_bytes(rank_mid.at[pl.ds(1, NY - 1)], yr_send)
    await_bytes(rank_got.at[pl.ds(0, NZ - 1)], zr_send)
    await_bytes(got.at[:, pl.ds(0, NZ - 1)], z_send)
    for j in range(4):
        await_bytes(got, x_send.at[j])
    for copy in halves:
        copy.wait_send()
    await_bytes(back.at[pl.ds(0, 7)], p_send)

    await_bytes(back.at[pl.ds(0, NZ - 1)], b_recv)
    total = jnp.zeros((1, ROWS), F32)
    for g, held in enumerate(collect(back)):
        one = held.astype(BF16).astype(F32)
        two = (held - one).astype(BF16).astype(F32)
        three = held - one - two
        row = iota((16, BIG), 0)
        split = jnp.where(row == 0, one, jnp.where(row == 1, two, jnp.where(row == 2, three, 0.0))).astype(BF16)
        picked = jnp.dot(split, place[g * BIG:(g + 1) * BIG, :], preferred_element_type=F32)
        total = total + (picked[0:1] + picked[1:2] + picked[2:3])
    out_ref[...] = total
    await_bytes(back.at[pl.ds(0, NZ - 1)], b_send)


def local(embeddings, cluster_ids, order_keys):
    dma = pltpu.SemaphoreType.DMA
    vmem = pltpu.VMEM
    out = pl.pallas_call(
        kernel,
        out_shape=jax.ShapeDtypeStruct((1, ROWS), F32),
        in_specs=[pl.BlockSpec(memory_space=pl.ANY)] * 3,
        out_specs=pl.BlockSpec(memory_space=vmem),
        scratch_shapes=[
            vmem((ROWS, D), BF16),
            vmem((1, ROWS), jnp.int32),
            vmem((1, ROWS), jnp.int32),
            vmem((NY * BIG, ROWS), BF16),
            vmem((NY, NZ, 16, D // 2), BF16),
            vmem((NY, NZ, 16, D // 2), BF16),
            vmem((NY, NZ, 16, D // 2), BF16),
            vmem((NY, 1, BIG), F32),
            vmem((NY, 1, BIG), F32),
            vmem((SUBS, 1, BIG), F32),
            vmem((NZ, 1, BIG), F32),
            vmem((5, NY, 1, BIG), F32),
            vmem((3, 5, BIG, D), BF16),
            vmem((2, 5, SMALL, D), BF16),
            vmem((4, 3, BIG, BIG), F32),
            vmem((16, 1, BIG), F32),
            vmem((16, 8, BIG), F32),
            vmem((4, NY, 1, BIG), F32),
            vmem((2, NY, 1, BIG), F32),
            vmem((2, NY, 1, BIG), F32),
            vmem((2, NY, 1, BIG), F32),
            vmem((SUBS, 1, BIG), F32),
            vmem((NZ, 1, BIG), F32),
            dma((3,)), pltpu.SemaphoreType.REGULAR((2, NZ // 2 + 1)), dma((NY,)), dma((NY,)), dma, dma, dma, dma((NY, SUBS)), dma, dma,
            dma((4,)), dma((4 * SUBS, 4)), dma((4,)), dma((4,)), dma((2,)), dma((2,)), dma, dma((2,)), dma, dma,
        ],
        compiler_params=pltpu.CompilerParams(collective_id=0, has_side_effects=True, vmem_limit_bytes=56 * 2**20),
    )(embeddings, cluster_ids.reshape(1, ROWS), order_keys.reshape(1, ROWS))
    return out.reshape(ROWS)


def solution(mesh):
    placed = (P(("shard", "slot"), None), P(("shard", "slot")), P(("shard", "slot")))
    return jax.shard_map(local, mesh=mesh, in_specs=placed, out_specs=P(("shard", "slot")), check_vma=False)
```

```python
import jax
import jax.numpy as jnp
from jax import lax
from jax.experimental import pallas as pl
from jax.experimental.pallas import tpu as pltpu
from jax.sharding import PartitionSpec as P

MESH = pl.DeviceIdType.MESH
F32, BF16 = jnp.float32, jnp.bfloat16
NX, NY, NZ = 4, 4, 16
D, CAP = 768, 8
ROWS = 256
BIG, SMALL = 128, 64
SUB = 4
SUBS = NZ // SUB
PLACES = SUB * CAP
AHEAD = 6
LAG = 2
NEVER = 1e9
ORDER = (0, 1, 3, 2)
A1, A0, L0, R0, R1 = range(5)
KEYS, QUERIES = (A0, L0, R0), (A1, A0, R0, R1)


def iota(shape, axis):
    return lax.broadcasted_iota(jnp.int32, shape, axis)


WAY = (1, 15, 2, 14, 3, 13, 4, 12, 5, 11, 6, 10, 7, 9, 8, 0)


def turn(rows):
    group = iota((1, 128), 1) // 32
    out = []
    for j in range(4):
        row = rows[0] if j == 0 else pltpu.roll(rows[0], (32 * (0 - j)) % 128, 1)
        for i in range(1, 4):
            shift = (32 * (i - j)) % 128
            row = jnp.where(group == i, rows[i] if shift == 0 else pltpu.roll(rows[i], shift, 1), row)
        out.append(row)
    return out


def collect(ref):
    held = ref[...].reshape(NZ, 128)
    held = jnp.where((iota((NZ, 128), 1) // CAP) % 4 == iota((NZ, 128), 0) % 4, held, 0.0)
    return turn([jnp.sum(held[4 * q:4 * q + 4], axis=0, keepdims=True) for q in range(4)])


def kernel(x_hbm, ids_hbm, keys_hbm, out_ref, x_ref, ids_ref, keys_ref, place, sent, stage, got, rank_out, rank_mid,
           rank_turned, rank_got, ranks, big, small, keyed, query, best, part, half, whole, other, turned, back,
           in_sem, ready, y_send, y_recv, yr_send, yr_recv, z_send, z_recv, zr_send, zr_recv, x_send, x_recv, xr_send, xr_recv,
           h_send, h_recv, p_send, p_recv, b_send, b_recv):
    shard, z = lax.axis_index("shard"), lax.axis_index("slot")
    x, y, core = shard // 8, (shard // 2) % 4, shard % 2

    def at(dx, dy, flip, dz):
        core_ = 1 - core if flip else core
        return ((((x + dx) % NX) * NY + (y + dy) % NY) * 2 + core_, (z + dz) % NZ)

    twin, right, left = at(0, 0, True, 0), at(1, 0, False, 0), at(3, 0, False, 0)

    def remote(src, dst, send, recv, device):
        return pltpu.make_async_remote_copy(src_ref=src, dst_ref=dst, send_sem=send, recv_sem=recv, device_id=device,
                                            device_id_type=MESH)

    def await_bytes(ref, sem):
        pltpu.make_async_copy(ref, ref, sem).wait()

    loads = [pltpu.make_async_copy(a, b, in_sem.at[i])
             for i, (a, b) in enumerate(((ids_hbm, ids_ref), (keys_hbm, keys_ref), (x_hbm, x_ref)))]
    for load in loads:
        load.start()

    barrier = pltpu.get_barrier_semaphore()

    def greet(device):
        pl.semaphore_signal(barrier, inc=1, device_id=device, device_id_type=MESH)

    def greet_z(d, carry):
        greet(at(0, 0, False, d))
        return carry

    above, below = at(0, 0, False, 1), at(0, 0, False, 15)
    for device in (twin, right, left, above, below):
        greet(device)
    for g in range(1, NY):
        greet(at(3, g, False, 0))
        greet(at(0, g, False, 0))

    loads[0].wait()
    ids = ids_ref[...]
    across = jnp.broadcast_to(ids.astype(F32), (ROWS, ROWS))
    before = (across == jnp.transpose(across)) & (iota((ROWS, ROWS), 0) < iota((ROWS, ROWS), 1))
    position = jnp.sum(jnp.where(before, 1.0, 0.0), axis=0, keepdims=True).astype(jnp.int32)
    step_y, step_z = ((ids & 3) + NY - y) & (NY - 1), ((ids >> 2) + NZ - z) & (NZ - 1)
    block = jnp.zeros_like(ids)
    for b in range(NZ):
        block = jnp.where(step_z == WAY[b], b, block)
    target = (step_y * NZ + block) * CAP + position
    place[...] = jnp.where(iota((NY * BIG, ROWS), 0) == target, 1.0, 0.0).astype(BF16)

    loads[1].wait()
    value = keys_ref[...] + 1
    upper = (value + 256) >> 9
    lower = value - upper * 512
    digits = jnp.where(iota((16, ROWS), 0) == 0, upper, jnp.where(iota((16, ROWS), 0) == 1, lower, 0))
    found = lax.dot_general(digits.astype(F32).astype(BF16), place[...], (((1,), (1,)), ((), ())), preferred_element_type=F32)
    value = found[0:1] * 512.0 + found[1:2]
    for g in range(NY):
        rank_out[g] = value[:, g * BIG:(g + 1) * BIG]

    loads[2].wait()
    wide = x_ref[...].astype(F32)
    unit = (wide * lax.rsqrt(jnp.sum(wide * wide, axis=1, keepdims=True) + 1e-6)).astype(BF16)
    for g in range(NY):
        laid = jnp.dot(place[g * BIG:(g + 1) * BIG, :], unit, preferred_element_type=F32)
        halves = [laid[:, :D // 2].reshape(NZ, CAP, D // 2), laid[:, D // 2:].reshape(NZ, CAP, D // 2)]
        sent[g] = jnp.concatenate(halves, axis=1).astype(BF16)

    pl.semaphore_wait(barrier, 11)

    def tell(d):
        pl.semaphore_signal(ready.at[0, d], inc=1, device_id=below, device_id_type=MESH)
        if d < NZ // 2:
            pl.semaphore_signal(ready.at[1, d], inc=1, device_id=above, device_id_type=MESH)

    def hear(d):
        pl.semaphore_wait(ready.at[0, d], 1)
        if d < NZ // 2:
            pl.semaphore_wait(ready.at[1, d], 1)
            tell(d + 1)

    tell(2)

    def along_z(n):
        i, sub = divmod(n, SUBS)
        g, source = ORDER[i], stage if i else sent
        if i and sub == 0:
            along_y[g].wait_recv()
        for b in range(sub * SUB, (sub + 1) * SUB):
            if i == 0 and b % 2 == 0 and b >= 2:
                hear(WAY[b])
            if WAY[b]:
                remote(source.at[g, b], got.at[g, b], z_send, z_recv.at[g, sub], at(0, 0, False, WAY[b])).start()
            else:
                got[g, b] = source[g, b]

    for g in ORDER[1:]:
        remote(rank_out.at[g], rank_mid.at[g], yr_send, yr_recv, at(0, g, False, 0)).start()
    along_y = {g: remote(sent.at[g], stage.at[g], y_send.at[g], y_recv.at[g], at(0, g, False, 0)) for g in ORDER[1:]}
    for g in ORDER[1:]:
        along_y[g].start()
    for n in range(SUBS):
        along_z(n)

    best[...] = jnp.full(best.shape, -1.0, F32)
    await_bytes(rank_mid.at[pl.ds(1, NY - 1)], yr_recv)
    for q, row in enumerate(turn([rank_out[0]] + [rank_mid[g] for g in range(1, NY)])):
        rank_turned[q] = row

    for b in reversed(range(NZ - 1)):
        remote(rank_turned.at[b // SUB], rank_got.at[b], zr_send, zr_recv, at(0, 0, False, WAY[b])).start()
    rank_got[NZ - 1] = rank_turned[SUBS - 1]
    for n in range(SUBS, AHEAD):
        along_z(n)

    shared = [remote(ranks.at[a], ranks.at[b], xr_send.at[i], xr_recv.at[i], device)
              for i, (a, b, device) in enumerate(((A0, R0, left), (A0, L0, right), (A0, A1, twin), (R0, R1, twin)))]

    def gather_ranks():
        await_bytes(rank_got.at[pl.ds(0, NZ - 1)], zr_recv)
        for g, row in enumerate(collect(rank_got)):
            ranks[A0, g] = row
        for copy in shared[:3]:
            copy.start()

    def rows_of(i, sub, a):
        if i < 3:
            return big.at[i, a, pl.ds(sub * PLACES, PLACES)]
        return small.at[sub // 2, a, pl.ds(sub % 2 * PLACES, PLACES)]

    def passed(i, sub, j):
        a, b, device = ((A0, R0, left), (A0, L0, right), (A0, A1, twin), (R0, R1, twin))[j]
        return remote(rows_of(i, sub, a), rows_of(i, sub, b), x_send.at[j], x_recv.at[i * SUBS + sub, j], device)

    def pass_on(i, sub):
        g = ORDER[i]
        first = sub * SUB
        count = SUB - 1 if sub == SUBS - 1 else SUB
        await_bytes(got.at[g, pl.ds(first, count)], z_recv.at[g, sub])
        held = got[g, first:first + SUB].astype(F32)
        rows = jnp.concatenate([held[:, :CAP].reshape(PLACES, D // 2), held[:, CAP:].reshape(PLACES, D // 2)], axis=1)
        rows_of(i, sub, A0)[...] = rows.astype(BF16)
        for j in range(3):
            passed(i, sub, j).start()

    def pass_twin(i, sub):
        passed(i, sub, 0).wait_recv()
        passed(i, sub, 3).start()

    def learn_ranks():
        for copy in shared[:3]:
            copy.wait_recv()
        shared[3].start()
        for i, g in enumerate(ORDER):
            for s, a in enumerate(KEYS):
                rank = ranks[a, g]
                rank = jnp.where(rank > 0.5, rank, NEVER)
                keyed[i, s] = jnp.transpose(jnp.broadcast_to(rank, (BIG, BIG)))
        shared[3].wait_recv()
        for i in range(3):
            for j, a in enumerate(QUERIES):
                query[4 * i + j] = ranks[a, ORDER[i]]
        low = iota((1, BIG), 1) < SMALL
        for s, (a, b) in enumerate(((A1, A0), (R0, R1))):
            one, two = ranks[a, ORDER[3]], ranks[b, ORDER[3]]
            query[12 + s] = jnp.where(low, one, pltpu.roll(two, SMALL, 1))
            query[14 + s] = jnp.where(low, pltpu.roll(one, SMALL, 1), two)

    def dots(k, q):
        return lax.dot_general(k, q, (((1,), (1,)), ((), ())), preferred_element_type=F32)

    def rows_in(p, a, b):
        if p >= 3:
            return small[p - 3, a:b].reshape((b - a) * SMALL, D)
        return big[p, a:b].reshape((b - a) * BIG, D)

    def key_ranks(p, s):
        if p >= 3:
            return keyed[3, s, (p - 3) * SMALL:(p - 2) * SMALL]
        return keyed[p, s]

    def groups(q, far):
        if q >= 3:
            return [12 + 2 * (q - 3) + far]
        return [4 * q + 2 * far, 4 * q + 2 * far + 1]

    def fold(sims, rank, j):
        masked = jnp.where(rank < query[j], sims, -1.0)
        best[j] = jnp.maximum(best[j], jnp.max(masked.reshape(sims.shape[0] // 8, 8, 128), axis=0))

    def inner(k, q):
        sims = dots(rows_in(k, A0, R1), rows_in(q, A1, L0))
        size = sims.shape[0] // 3
        for s in range(3):
            for n, j in enumerate(groups(q, 0)):
                fold(sims[s * size:(s + 1) * size, n * 128:(n + 1) * 128], key_ranks(k, s), j)

    def outer(k, q):
        sims = dots(rows_in(k, L0, R0), rows_in(q, R0, R1 + 1))
        for n, j in enumerate(groups(q, 1)):
            fold(sims[:, n * 128:(n + 1) * 128], key_ranks(k, 1), j)

    def pairs(p, work):
        for h in range(min(p, 3)):
            work(h, p)
            work(p, h)
        if p == 4:
            work(3, 4)
            work(4, 3)
        work(p, p)

    def subs_of(p):
        return [(p, sub) for sub in range(SUBS)] if p < 3 else [(3, 2 * (p - 3)), (3, 2 * (p - 3) + 1)]

    def compare_inner(p):
        for i, sub in subs_of(p):
            passed(i, sub, 2).wait_recv()
            passed(i, sub, 1).wait_recv()
        pairs(p, inner)

    def compare_outer(p):
        for i, sub in subs_of(p):
            passed(i, sub, 3).wait_recv()
        pairs(p, outer)

    for n in range(4 * SUBS):
        pass_on(n // SUBS, n % SUBS)
        if n + AHEAD < 4 * SUBS:
            along_z(n + AHEAD)
        if n == 1:
            gather_ranks()
        if n == SUBS:
            learn_ranks()
        if n >= LAG:
            pass_twin((n - LAG) // SUBS, (n - LAG) % SUBS)
        i, sub = divmod(n - LAG, SUBS)
        if sub == SUBS - 1 and 0 <= i < 3:
            compare_inner(i)
        if sub == 0 and 0 < i < 4:
            compare_outer(i - 1)
    compare_inner(3)
    compare_outer(3)
    for n in range(4 * SUBS - LAG, 4 * SUBS):
        pass_twin(n // SUBS, n % SUBS)
    compare_inner(4)
    compare_outer(4)

    low = iota((1, BIG), 1) < SMALL
    top = [jnp.max(best[j], axis=0, keepdims=True) for j in range(16)]
    for j, a in enumerate(QUERIES):
        for i in range(3):
            part[a, ORDER[i]] = top[4 * i + j]
        one, two = top[12 + j // 2], top[14 + j // 2]
        part[a, ORDER[3]] = (jnp.where(low, one, pltpu.roll(two, SMALL, 1)) if a in (A1, R0) else
                             jnp.where(low, pltpu.roll(one, SMALL, 1), two))
    halves = [remote(part.at[a], half.at[i], h_send.at[i], h_recv.at[i], twin) for i, a in enumerate((R1, A1))]
    for copy in halves:
        copy.start()
    for n, (a, dx) in enumerate(((R0, 1), (A0, 0))):
        halves[n].wait_recv()
        for g in (2, 1, 3, 0):
            whole[n, g] = jnp.maximum(part[a, g], half[n, g])
            if dx or g:
                remote(whole.at[n, g], other.at[n, g], p_send, p_recv.at[n], at(dx, NY - g, False, 0)).start()
    other[1, 0] = whole[1, 0]
    await_bytes(other.at[0], p_recv.at[0])
    await_bytes(other.at[1, pl.ds(1, 3)], p_recv.at[1])
    most = [jnp.maximum(other[0, g], other[1, g]) for g in range(NY)]
    for q, row in enumerate(turn(most)):
        turned[q] = row

    for b in reversed(range(NZ - 1)):
        remote(turned.at[b // SUB], back.at[b], b_send, b_recv, at(0, 0, False, NZ - WAY[b])).start()
    back[NZ - 1] = turned[SUBS - 1]

    for g in ORDER[1:]:
        along_y[g].wait_send()
    for copy in shared:
        copy.wait_send()
    await_bytes(rank_mid.at[pl.ds(1, NY - 1)], yr_send)
    await_bytes(rank_got.at[pl.ds(0, NZ - 1)], zr_send)
    await_bytes(got.at[:, pl.ds(0, NZ - 1)], z_send)
    for j in range(4):
        await_bytes(got, x_send.at[j])
    for copy in halves:
        copy.wait_send()
    await_bytes(back.at[pl.ds(0, 7)], p_send)

    await_bytes(back.at[pl.ds(0, NZ - 1)], b_recv)
    total = jnp.zeros((1, ROWS), F32)
    for g, held in enumerate(collect(back)):
        one = held.astype(BF16).astype(F32)
        two = (held - one).astype(BF16).astype(F32)
        three = held - one - two
        row = iota((16, BIG), 0)
        split = jnp.where(row == 0, one, jnp.where(row == 1, two, jnp.where(row == 2, three, 0.0))).astype(BF16)
        picked = jnp.dot(split, place[g * BIG:(g + 1) * BIG, :], preferred_element_type=F32)
        total = total + (picked[0:1] + picked[1:2] + picked[2:3])
    out_ref[...] = total.reshape(ROWS)
    await_bytes(back.at[pl.ds(0, NZ - 1)], b_send)


def local(embeddings, cluster_ids, order_keys):
    dma = pltpu.SemaphoreType.DMA
    vmem = pltpu.VMEM
    out = pl.pallas_call(
        kernel,
        out_shape=jax.ShapeDtypeStruct((ROWS,), F32),
        in_specs=[pl.BlockSpec(memory_space=pl.ANY)] * 3,
        out_specs=pl.BlockSpec(memory_space=vmem),
        scratch_shapes=[
            vmem((ROWS, D), BF16),
            vmem((1, ROWS), jnp.int32),
            vmem((1, ROWS), jnp.int32),
            vmem((NY * BIG, ROWS), BF16),
            vmem((NY, NZ, 16, D // 2), BF16),
            vmem((NY, NZ, 16, D // 2), BF16),
            vmem((NY, NZ, 16, D // 2), BF16),
            vmem((NY, 1, BIG), F32),
            vmem((NY, 1, BIG), F32),
            vmem((SUBS, 1, BIG), F32),
            vmem((NZ, 1, BIG), F32),
            vmem((5, NY, 1, BIG), F32),
            vmem((3, 5, BIG, D), BF16),
            vmem((2, 5, SMALL, D), BF16),
            vmem((4, 3, BIG, BIG), F32),
            vmem((16, 1, BIG), F32),
            vmem((16, 8, BIG), F32),
            vmem((5, NY, 1, BIG), F32),
            vmem((2, NY, 1, BIG), F32),
            vmem((2, NY, 1, BIG), F32),
            vmem((2, NY, 1, BIG), F32),
            vmem((SUBS, 1, BIG), F32),
            vmem((NZ, 1, BIG), F32),
            dma((3,)), pltpu.SemaphoreType.REGULAR((2, NZ // 2 + 1)), dma((NY,)), dma((NY,)), dma, dma, dma, dma((NY, SUBS)), dma, dma,
            dma((4,)), dma((4 * SUBS, 4)), dma((4,)), dma((4,)), dma((2,)), dma((2,)), dma, dma((2,)), dma, dma,
        ],
        compiler_params=pltpu.CompilerParams(collective_id=0, has_side_effects=True, vmem_limit_bytes=56 * 2**20),
    )(embeddings, cluster_ids.reshape(1, ROWS), order_keys.reshape(1, ROWS))
    return out


def solution(mesh):
    placed = (P(("shard", "slot"), None), P(("shard", "slot")), P(("shard", "slot")))
    return jax.shard_map(local, mesh=mesh, in_specs=placed, out_specs=P(("shard", "slot")), check_vma=False)
```

```python
import jax
import jax.numpy as jnp
from jax import lax
from jax.experimental import pallas as pl
from jax.experimental.pallas import tpu as pltpu
from jax.sharding import PartitionSpec as P

MESH = pl.DeviceIdType.MESH
F32, BF16 = jnp.float32, jnp.bfloat16
NX, NY, NZ = 4, 4, 16
D, CAP = 768, 8
ROWS = 256
BIG, SMALL = 128, 64
SUB = 4
SUBS = NZ // SUB
PLACES = SUB * CAP
AHEAD = 6
LAG = 2
NEVER = 1e9
ORDER = (0, 1, 3, 2)
A1, A0, L0, R0, R1 = range(5)
KEYS, QUERIES = (A0, L0, R0), (A1, A0, R0, R1)


def iota(shape, axis):
    return lax.broadcasted_iota(jnp.int32, shape, axis)


WAY = (1, 15, 2, 14, 3, 13, 4, 12, 5, 11, 6, 10, 7, 9, 8, 0)


def turn(rows):
    group = iota((1, 128), 1) // 32
    out = []
    for j in range(4):
        row = rows[0] if j == 0 else pltpu.roll(rows[0], (32 * (0 - j)) % 128, 1)
        for i in range(1, 4):
            shift = (32 * (i - j)) % 128
            row = jnp.where(group == i, rows[i] if shift == 0 else pltpu.roll(rows[i], shift, 1), row)
        out.append(row)
    return out


def collect(ref):
    held = ref[...].reshape(NZ, 128)
    held = jnp.where((iota((NZ, 128), 1) // CAP) % 4 == iota((NZ, 128), 0) % 4, held, 0.0)
    return turn([jnp.sum(held[4 * q:4 * q + 4], axis=0, keepdims=True) for q in range(4)])


def kernel(x_hbm, ids_hbm, keys_hbm, out_ref, x_ref, ids_ref, keys_ref, place, sent, stage, got, rank_out, rank_mid,
           rank_turned, rank_got, ranks, big, small, keyed, query, best, part, half, whole, other, turned, back,
           in_sem, ready, y_send, y_recv, yr_send, yr_recv, z_send, z_recv, zr_send, zr_recv, x_send, x_recv, xr_send, xr_recv,
           h_send, h_recv, p_send, p_recv, b_send, b_recv):
    shard, z = lax.axis_index("shard"), lax.axis_index("slot")
    x, y, core = shard // 8, (shard // 2) % 4, shard % 2

    def at(dx, dy, flip, dz):
        core_ = 1 - core if flip else core
        return ((((x + dx) % NX) * NY + (y + dy) % NY) * 2 + core_, (z + dz) % NZ)

    twin, right, left = at(0, 0, True, 0), at(1, 0, False, 0), at(3, 0, False, 0)

    def remote(src, dst, send, recv, device):
        return pltpu.make_async_remote_copy(src_ref=src, dst_ref=dst, send_sem=send, recv_sem=recv, device_id=device,
                                            device_id_type=MESH)

    def await_bytes(ref, sem):
        pltpu.make_async_copy(ref, ref, sem).wait()

    loads = [pltpu.make_async_copy(a, b, in_sem.at[i])
             for i, (a, b) in enumerate(((ids_hbm, ids_ref), (keys_hbm, keys_ref), (x_hbm, x_ref)))]
    for load in loads:
        load.start()

    barrier = pltpu.get_barrier_semaphore()

    def greet(device):
        pl.semaphore_signal(barrier, inc=1, device_id=device, device_id_type=MESH)

    def greet_z(d, carry):
        greet(at(0, 0, False, d))
        return carry

    above, below = at(0, 0, False, 1), at(0, 0, False, 15)
    for device in (twin, right, left, above, below):
        greet(device)
    for g in range(1, NY):
        greet(at(3, g, False, 0))
        greet(at(0, g, False, 0))

    loads[0].wait()
    ids = ids_ref[...]
    across = jnp.broadcast_to(ids.astype(F32), (ROWS, ROWS))
    before = (across == jnp.transpose(across)) & (iota((ROWS, ROWS), 0) < iota((ROWS, ROWS), 1))
    position = jnp.sum(jnp.where(before, 1.0, 0.0), axis=0, keepdims=True).astype(jnp.int32)
    step_y, step_z = ((ids & 3) + NY - y) & (NY - 1), ((ids >> 2) + NZ - z) & (NZ - 1)
    block = jnp.zeros_like(ids)
    for b in range(NZ):
        block = jnp.where(step_z == WAY[b], b, block)
    target = (step_y * NZ + block) * CAP + position
    place[...] = jnp.where(iota((NY * BIG, ROWS), 0) == target, 1.0, 0.0).astype(BF16)

    loads[1].wait()
    value = keys_ref[...] + 1
    upper = (value + 256) >> 9
    lower = value - upper * 512
    digits = jnp.where(iota((16, ROWS), 0) == 0, upper, jnp.where(iota((16, ROWS), 0) == 1, lower, 0))
    found = lax.dot_general(digits.astype(F32).astype(BF16), place[...], (((1,), (1,)), ((), ())), preferred_element_type=F32)
    value = found[0:1] * 512.0 + found[1:2]
    for g in range(NY):
        rank_out[g] = value[:, g * BIG:(g + 1) * BIG]

    loads[2].wait()
    wide = x_ref[...].astype(F32)
    unit = (wide * lax.rsqrt(jnp.sum(wide * wide, axis=1, keepdims=True) + 1e-6)).astype(BF16)
    for g in range(NY):
        laid = jnp.dot(place[g * BIG:(g + 1) * BIG, :], unit, preferred_element_type=F32)
        halves = [laid[:, :D // 2].reshape(NZ, CAP, D // 2), laid[:, D // 2:].reshape(NZ, CAP, D // 2)]
        sent[g] = jnp.concatenate(halves, axis=1).astype(BF16)

    pl.semaphore_wait(barrier, 11)

    def tell(d):
        pl.semaphore_signal(ready.at[0, d], inc=1, device_id=below, device_id_type=MESH)
        if d < NZ // 2:
            pl.semaphore_signal(ready.at[1, d], inc=1, device_id=above, device_id_type=MESH)

    def hear(d):
        pl.semaphore_wait(ready.at[0, d], 1)
        if d < NZ // 2:
            pl.semaphore_wait(ready.at[1, d], 1)
            tell(d + 1)

    tell(2)

    def along_z(n):
        i, sub = divmod(n, SUBS)
        g, source = ORDER[i], stage if i else sent
        if i and sub == 0:
            along_y[g].wait_recv()
        for b in range(sub * SUB, (sub + 1) * SUB):
            if i == 0 and b % 2 == 0 and b >= 2:
                hear(WAY[b])
            if WAY[b]:
                remote(source.at[g, b], got.at[g, b], z_send, z_recv.at[g, sub], at(0, 0, False, WAY[b])).start()
            else:
                got[g, b] = source[g, b]

    for g in ORDER[1:]:
        remote(rank_out.at[g], rank_mid.at[g], yr_send, yr_recv, at(0, g, False, 0)).start()
    along_y = {g: remote(sent.at[g], stage.at[g], y_send.at[g], y_recv.at[g], at(0, g, False, 0)) for g in ORDER[1:]}
    for g in ORDER[1:]:
        along_y[g].start()
    for n in range(SUBS):
        along_z(n)

    best[...] = jnp.full(best.shape, -1.0, F32)
    await_bytes(rank_mid.at[pl.ds(1, NY - 1)], yr_recv)
    for q, row in enumerate(turn([rank_out[0]] + [rank_mid[g] for g in range(1, NY)])):
        rank_turned[q] = row

    for b in reversed(range(NZ - 1)):
        remote(rank_turned.at[b // SUB], rank_got.at[b], zr_send, zr_recv, at(0, 0, False, WAY[b])).start()
    rank_got[NZ - 1] = rank_turned[SUBS - 1]
    for n in range(SUBS, AHEAD):
        along_z(n)

    shared = [remote(ranks.at[a], ranks.at[b], xr_send.at[i], xr_recv.at[i], device)
              for i, (a, b, device) in enumerate(((A0, R0, left), (A0, L0, right), (A0, A1, twin), (R0, R1, twin)))]

    def gather_ranks():
        await_bytes(rank_got.at[pl.ds(0, NZ - 1)], zr_recv)
        for g, row in enumerate(collect(rank_got)):
            ranks[A0, g] = row
        for copy in shared[:3]:
            copy.start()

    def rows_of(i, sub, a):
        if i < 3:
            return big.at[i, a, pl.ds(sub * PLACES, PLACES)]
        return small.at[sub // 2, a, pl.ds(sub % 2 * PLACES, PLACES)]

    def passed(i, sub, j):
        a, b, device = ((A0, R0, left), (A0, L0, right), (A0, A1, twin), (R0, R1, twin))[j]
        return remote(rows_of(i, sub, a), rows_of(i, sub, b), x_send.at[j], x_recv.at[i * SUBS + sub, j], device)

    def pass_on(i, sub):
        g = ORDER[i]
        first = sub * SUB
        count = SUB - 1 if sub == SUBS - 1 else SUB
        await_bytes(got.at[g, pl.ds(first, count)], z_recv.at[g, sub])
        held = got[g, first:first + SUB].astype(F32)
        rows = jnp.concatenate([held[:, :CAP].reshape(PLACES, D // 2), held[:, CAP:].reshape(PLACES, D // 2)], axis=1)
        rows_of(i, sub, A0)[...] = rows.astype(BF16)
        for j in range(3):
            passed(i, sub, j).start()

    def pass_twin(i, sub):
        passed(i, sub, 0).wait_recv()
        passed(i, sub, 3).start()

    def learn_ranks():
        for copy in shared[:3]:
            copy.wait_recv()
        shared[3].start()
        for i, g in enumerate(ORDER):
            for s, a in enumerate(KEYS):
                rank = ranks[a, g]
                rank = jnp.where(rank > 0.5, rank, NEVER)
                keyed[i, s] = jnp.transpose(jnp.broadcast_to(rank, (BIG, BIG)))
        shared[3].wait_recv()
        for i in range(3):
            for j, a in enumerate(QUERIES):
                query[4 * i + j] = ranks[a, ORDER[i]]
        low = iota((1, BIG), 1) < SMALL
        for s, (a, b) in enumerate(((A1, A0), (R0, R1))):
            one, two = ranks[a, ORDER[3]], ranks[b, ORDER[3]]
            query[12 + s] = jnp.where(low, one, pltpu.roll(two, SMALL, 1))
            query[14 + s] = jnp.where(low, pltpu.roll(one, SMALL, 1), two)

    def dots(k, q):
        return lax.dot_general(k, q, (((1,), (1,)), ((), ())), preferred_element_type=F32)

    def rows_in(p, a, b):
        if p >= 3:
            return small[p - 3, a:b].reshape((b - a) * SMALL, D)
        return big[p, a:b].reshape((b - a) * BIG, D)

    def key_ranks(p, s):
        if p >= 3:
            return keyed[3, s, (p - 3) * SMALL:(p - 2) * SMALL]
        return keyed[p, s]

    def groups(q, far):
        if q >= 3:
            return [12 + 2 * (q - 3) + far]
        return [4 * q + 2 * far, 4 * q + 2 * far + 1]

    def fold(sims, rank, j):
        masked = jnp.where(rank < query[j], sims, -1.0)
        best[j] = jnp.maximum(best[j], jnp.max(masked.reshape(sims.shape[0] // 8, 8, 128), axis=0))

    def inner(k, q):
        sims = dots(rows_in(k, A0, R1), rows_in(q, A1, L0))
        size = sims.shape[0] // 3
        for s in range(3):
            for n, j in enumerate(groups(q, 0)):
                fold(sims[s * size:(s + 1) * size, n * 128:(n + 1) * 128], key_ranks(k, s), j)

    def own(k, q):
        sims = dots(rows_in(k, A0, L0), rows_in(q, A1, L0))
        for n, j in enumerate(groups(q, 0)):
            fold(sims[:, n * 128:(n + 1) * 128], key_ranks(k, 0), j)

    def beside(k, q):
        sims = dots(rows_in(k, L0, R1), rows_in(q, A1, L0))
        size = sims.shape[0] // 2
        for s in range(2):
            for n, j in enumerate(groups(q, 0)):
                fold(sims[s * size:(s + 1) * size, n * 128:(n + 1) * 128], key_ranks(k, 1 + s), j)

    def outer(k, q):
        sims = dots(rows_in(k, L0, R0), rows_in(q, R0, R1 + 1))
        for n, j in enumerate(groups(q, 1)):
            fold(sims[:, n * 128:(n + 1) * 128], key_ranks(k, 1), j)

    def pairs(p, work):
        for h in range(min(p, 3)):
            work(h, p)
            work(p, h)
        if p == 4:
            work(3, 4)
            work(4, 3)
        work(p, p)

    def subs_of(p):
        return [(p, sub) for sub in range(SUBS)] if p < 3 else [(3, 2 * (p - 3)), (3, 2 * (p - 3) + 1)]

    def compare_inner(p):
        for i, sub in subs_of(p):
            passed(i, sub, 2).wait_recv()
            passed(i, sub, 1).wait_recv()
        pairs(p, inner)

    def compare_outer(p):
        for i, sub in subs_of(p):
            passed(i, sub, 3).wait_recv()
        pairs(p, outer)

    for n in range(4 * SUBS):
        pass_on(n // SUBS, n % SUBS)
        if n + AHEAD < 4 * SUBS:
            along_z(n + AHEAD)
        if n == 1:
            gather_ranks()
        if n == SUBS:
            learn_ranks()
        if n >= LAG:
            pass_twin((n - LAG) // SUBS, (n - LAG) % SUBS)
        i, sub = divmod(n - LAG, SUBS)
        if sub == SUBS - 1 and 0 <= i < 3:
            compare_inner(i)
        if sub == 0 and 0 < i < 4:
            compare_outer(i - 1)
    compare_inner(3)
    compare_outer(3)
    pass_twin(3, 2)
    for i, sub in subs_of(4):
        passed(i, sub, 2).wait_recv()
    pairs(4, own)
    pass_twin(3, 3)
    for i, sub in subs_of(4):
        passed(i, sub, 1).wait_recv()
    pairs(4, beside)

    low = iota((1, BIG), 1) < SMALL

    def gather_top(one_set):
        for j in (2 * one_set, 2 * one_set + 1):
            a = QUERIES[j]
            for i in range(3):
                part[a, ORDER[i]] = jnp.max(best[4 * i + j], axis=0, keepdims=True)
            one, two = [jnp.max(best[m + one_set], axis=0, keepdims=True) for m in (12, 14)]
            part[a, ORDER[3]] = (jnp.where(low, one, pltpu.roll(two, SMALL, 1)) if a in (A1, R0) else
                                 jnp.where(low, pltpu.roll(one, SMALL, 1), two))

    halves = [remote(part.at[a], half.at[i], h_send.at[i], h_recv.at[i], twin) for i, a in enumerate((R1, A1))]
    gather_top(0)
    halves[1].start()
    compare_outer(4)
    gather_top(1)
    halves[0].start()
    for n, (a, dx) in enumerate(((R0, 1), (A0, 0))):
        halves[n].wait_recv()
        for g in (2, 1, 3, 0):
            whole[n, g] = jnp.maximum(part[a, g], half[n, g])
            if dx or g:
                remote(whole.at[n, g], other.at[n, g], p_send, p_recv.at[n], at(dx, NY - g, False, 0)).start()
    other[1, 0] = whole[1, 0]
    await_bytes(other.at[0], p_recv.at[0])
    await_bytes(other.at[1, pl.ds(1, 3)], p_recv.at[1])
    most = [jnp.maximum(other[0, g], other[1, g]) for g in range(NY)]
    for q, row in enumerate(turn(most)):
        turned[q] = row

    for b in reversed(range(NZ - 1)):
        remote(turned.at[b // SUB], back.at[b], b_send, b_recv, at(0, 0, False, NZ - WAY[b])).start()
    back[NZ - 1] = turned[SUBS - 1]

    for g in ORDER[1:]:
        along_y[g].wait_send()
    for copy in shared:
        copy.wait_send()
    await_bytes(rank_mid.at[pl.ds(1, NY - 1)], yr_send)
    await_bytes(rank_got.at[pl.ds(0, NZ - 1)], zr_send)
    await_bytes(got.at[:, pl.ds(0, NZ - 1)], z_send)
    for j in range(4):
        await_bytes(got, x_send.at[j])
    for copy in halves:
        copy.wait_send()
    await_bytes(back.at[pl.ds(0, 7)], p_send)

    await_bytes(back.at[pl.ds(0, NZ - 1)], b_recv)
    total = jnp.zeros((1, ROWS), F32)
    for g, held in enumerate(collect(back)):
        one = held.astype(BF16).astype(F32)
        two = (held - one).astype(BF16).astype(F32)
        three = held - one - two
        row = iota((16, BIG), 0)
        split = jnp.where(row == 0, one, jnp.where(row == 1, two, jnp.where(row == 2, three, 0.0))).astype(BF16)
        picked = jnp.dot(split, place[g * BIG:(g + 1) * BIG, :], preferred_element_type=F32)
        total = total + (picked[0:1] + picked[1:2] + picked[2:3])
    out_ref[...] = total.reshape(ROWS)
    await_bytes(back.at[pl.ds(0, NZ - 1)], b_send)


def local(embeddings, cluster_ids, order_keys):
    dma = pltpu.SemaphoreType.DMA
    vmem = pltpu.VMEM
    out = pl.pallas_call(
        kernel,
        out_shape=jax.ShapeDtypeStruct((ROWS,), F32),
        in_specs=[pl.BlockSpec(memory_space=pl.ANY)] * 3,
        out_specs=pl.BlockSpec(memory_space=vmem),
        scratch_shapes=[
            vmem((ROWS, D), BF16),
            vmem((1, ROWS), jnp.int32),
            vmem((1, ROWS), jnp.int32),
            vmem((NY * BIG, ROWS), BF16),
            vmem((NY, NZ, 16, D // 2), BF16),
            vmem((NY, NZ, 16, D // 2), BF16),
            vmem((NY, NZ, 16, D // 2), BF16),
            vmem((NY, 1, BIG), F32),
            vmem((NY, 1, BIG), F32),
            vmem((SUBS, 1, BIG), F32),
            vmem((NZ, 1, BIG), F32),
            vmem((5, NY, 1, BIG), F32),
            vmem((3, 5, BIG, D), BF16),
            vmem((2, 5, SMALL, D), BF16),
            vmem((4, 3, BIG, BIG), F32),
            vmem((16, 1, BIG), F32),
            vmem((16, 8, BIG), F32),
            vmem((5, NY, 1, BIG), F32),
            vmem((2, NY, 1, BIG), F32),
            vmem((2, NY, 1, BIG), F32),
            vmem((2, NY, 1, BIG), F32),
            vmem((SUBS, 1, BIG), F32),
            vmem((NZ, 1, BIG), F32),
            dma((3,)), pltpu.SemaphoreType.REGULAR((2, NZ // 2 + 1)), dma((NY,)), dma((NY,)), dma, dma, dma, dma((NY, SUBS)), dma, dma,
            dma((4,)), dma((4 * SUBS, 4)), dma((4,)), dma((4,)), dma((2,)), dma((2,)), dma, dma((2,)), dma, dma,
        ],
        compiler_params=pltpu.CompilerParams(collective_id=0, has_side_effects=True, vmem_limit_bytes=56 * 2**20),
    )(embeddings, cluster_ids.reshape(1, ROWS), order_keys.reshape(1, ROWS))
    return out


def solution(mesh):
    placed = (P(("shard", "slot"), None), P(("shard", "slot")), P(("shard", "slot")))
    return jax.shard_map(local, mesh=mesh, in_specs=placed, out_specs=P(("shard", "slot")), check_vma=False)
```

```python
import jax
import jax.numpy as jnp
from jax import lax
from jax.experimental import pallas as pl
from jax.experimental.pallas import tpu as pltpu
from jax.sharding import PartitionSpec as P

MESH = pl.DeviceIdType.MESH
F32, BF16 = jnp.float32, jnp.bfloat16
NX, NY, NZ = 4, 4, 16
D, CAP = 768, 8
ROWS = 256
BIG, SMALL = 128, 64
SUB = 4
SUBS = NZ // SUB
PLACES = SUB * CAP
AHEAD = 7
LAG = 2
NEVER = 1e9
ORDER = (0, 1, 3, 2)
A1, A0, L0, R0, R1 = range(5)
KEYS, QUERIES = (A0, L0, R0), (A1, A0, R0, R1)


def iota(shape, axis):
    return lax.broadcasted_iota(jnp.int32, shape, axis)


WAY = (1, 15, 2, 14, 3, 13, 4, 12, 5, 11, 6, 10, 7, 9, 8, 0)


def turn(rows):
    group = iota((1, 128), 1) // 32
    out = []
    for j in range(4):
        row = rows[0] if j == 0 else pltpu.roll(rows[0], (32 * (0 - j)) % 128, 1)
        for i in range(1, 4):
            shift = (32 * (i - j)) % 128
            row = jnp.where(group == i, rows[i] if shift == 0 else pltpu.roll(rows[i], shift, 1), row)
        out.append(row)
    return out


def collect(ref):
    held = ref[...].reshape(NZ, 128)
    held = jnp.where((iota((NZ, 128), 1) // CAP) % 4 == iota((NZ, 128), 0) % 4, held, 0.0)
    return turn([jnp.sum(held[4 * q:4 * q + 4], axis=0, keepdims=True) for q in range(4)])


def kernel(x_hbm, ids_hbm, keys_hbm, out_ref, x_ref, ids_ref, keys_ref, place, sent, stage, got, rank_out, rank_mid,
           rank_turned, rank_got, ranks, big, small, keyed, query, best, part, half, whole, other, turned, back,
           in_sem, ready, y_send, y_recv, yr_send, yr_recv, z_send, z_recv, zr_send, zr_recv, x_send, x_recv, xr_send, xr_recv,
           h_send, h_recv, p_send, p_recv, b_send, b_recv):
    shard, z = lax.axis_index("shard"), lax.axis_index("slot")
    x, y, core = shard // 8, (shard // 2) % 4, shard % 2

    def at(dx, dy, flip, dz):
        core_ = 1 - core if flip else core
        return ((((x + dx) % NX) * NY + (y + dy) % NY) * 2 + core_, (z + dz) % NZ)

    twin, right, left = at(0, 0, True, 0), at(1, 0, False, 0), at(3, 0, False, 0)

    def remote(src, dst, send, recv, device):
        return pltpu.make_async_remote_copy(src_ref=src, dst_ref=dst, send_sem=send, recv_sem=recv, device_id=device,
                                            device_id_type=MESH)

    def await_bytes(ref, sem):
        pltpu.make_async_copy(ref, ref, sem).wait()

    loads = [pltpu.make_async_copy(a, b, in_sem.at[i])
             for i, (a, b) in enumerate(((ids_hbm, ids_ref), (keys_hbm, keys_ref), (x_hbm, x_ref)))]
    for load in loads:
        load.start()

    barrier = pltpu.get_barrier_semaphore()

    def greet(device):
        pl.semaphore_signal(barrier, inc=1, device_id=device, device_id_type=MESH)

    def greet_z(d, carry):
        greet(at(0, 0, False, d))
        return carry

    above, below = at(0, 0, False, 1), at(0, 0, False, 15)
    for device in (twin, right, left, above, below):
        greet(device)
    for g in range(1, NY):
        greet(at(3, g, False, 0))
        greet(at(0, g, False, 0))

    loads[0].wait()
    ids = ids_ref[...]
    across = jnp.broadcast_to(ids.astype(F32), (ROWS, ROWS))
    before = (across == jnp.transpose(across)) & (iota((ROWS, ROWS), 0) < iota((ROWS, ROWS), 1))
    position = jnp.sum(jnp.where(before, 1.0, 0.0), axis=0, keepdims=True).astype(jnp.int32)
    step_y, step_z = ((ids & 3) + NY - y) & (NY - 1), ((ids >> 2) + NZ - z) & (NZ - 1)
    block = jnp.zeros_like(ids)
    for b in range(NZ):
        block = jnp.where(step_z == WAY[b], b, block)
    target = (step_y * NZ + block) * CAP + position
    place[...] = jnp.where(iota((NY * BIG, ROWS), 0) == target, 1.0, 0.0).astype(BF16)

    loads[1].wait()
    value = keys_ref[...] + 1
    upper = (value + 256) >> 9
    lower = value - upper * 512
    digits = jnp.where(iota((16, ROWS), 0) == 0, upper, jnp.where(iota((16, ROWS), 0) == 1, lower, 0))
    found = lax.dot_general(digits.astype(F32).astype(BF16), place[...], (((1,), (1,)), ((), ())), preferred_element_type=F32)
    value = found[0:1] * 512.0 + found[1:2]
    for g in range(NY):
        rank_out[g] = value[:, g * BIG:(g + 1) * BIG]

    loads[2].wait()
    wide = x_ref[...].astype(F32)
    unit = (wide * lax.rsqrt(jnp.sum(wide * wide, axis=1, keepdims=True) + 1e-6)).astype(BF16)
    for g in range(NY):
        laid = jnp.dot(place[g * BIG:(g + 1) * BIG, :], unit, preferred_element_type=F32)
        halves = [laid[:, :D // 2].reshape(NZ, CAP, D // 2), laid[:, D // 2:].reshape(NZ, CAP, D // 2)]
        sent[g] = jnp.concatenate(halves, axis=1).astype(BF16)

    pl.semaphore_wait(barrier, 11)

    def tell(d):
        pl.semaphore_signal(ready.at[0, d], inc=1, device_id=below, device_id_type=MESH)
        if d < NZ // 2:
            pl.semaphore_signal(ready.at[1, d], inc=1, device_id=above, device_id_type=MESH)

    def hear(d):
        pl.semaphore_wait(ready.at[0, d], 1)
        if d < NZ // 2:
            pl.semaphore_wait(ready.at[1, d], 1)
            tell(d + 1)

    tell(2)

    def along_z(n):
        i, sub = divmod(n, SUBS)
        g, source = ORDER[i], stage if i else sent
        if i and sub == 0:
            along_y[g].wait_recv()
        for b in range(sub * SUB, (sub + 1) * SUB):
            if i == 0 and b % 2 == 0 and b >= 2:
                hear(WAY[b])
            if WAY[b]:
                remote(source.at[g, b], got.at[g, b], z_send, z_recv.at[g, sub], at(0, 0, False, WAY[b])).start()
            else:
                got[g, b] = source[g, b]

    for g in ORDER[1:]:
        remote(rank_out.at[g], rank_mid.at[g], yr_send, yr_recv, at(0, g, False, 0)).start()
    along_y = {g: remote(sent.at[g], stage.at[g], y_send.at[g], y_recv.at[g], at(0, g, False, 0)) for g in ORDER[1:]}
    for g in ORDER[1:]:
        along_y[g].start()
    for n in range(SUBS):
        along_z(n)

    best[...] = jnp.full(best.shape, -1.0, F32)
    await_bytes(rank_mid.at[pl.ds(1, NY - 1)], yr_recv)
    for q, row in enumerate(turn([rank_out[0]] + [rank_mid[g] for g in range(1, NY)])):
        rank_turned[q] = row

    for b in reversed(range(NZ - 1)):
        remote(rank_turned.at[b // SUB], rank_got.at[b], zr_send, zr_recv, at(0, 0, False, WAY[b])).start()
    rank_got[NZ - 1] = rank_turned[SUBS - 1]
    for n in range(SUBS, AHEAD):
        along_z(n)

    shared = [remote(ranks.at[a], ranks.at[b], xr_send.at[i], xr_recv.at[i], device)
              for i, (a, b, device) in enumerate(((A0, R0, left), (A0, L0, right), (A0, A1, twin), (R0, R1, twin)))]

    def gather_ranks():
        await_bytes(rank_got.at[pl.ds(0, NZ - 1)], zr_recv)
        for g, row in enumerate(collect(rank_got)):
            ranks[A0, g] = row
        for copy in shared[:3]:
            copy.start()

    def rows_of(i, sub, a):
        if i < 3:
            return big.at[i, a, pl.ds(sub * PLACES, PLACES)]
        return small.at[sub // 2, a, pl.ds(sub % 2 * PLACES, PLACES)]

    def passed(i, sub, j):
        a, b, device = ((A0, R0, left), (A0, L0, right), (A0, A1, twin), (R0, R1, twin))[j]
        return remote(rows_of(i, sub, a), rows_of(i, sub, b), x_send.at[j], x_recv.at[i * SUBS + sub, j], device)

    def pass_on(i, sub):
        g = ORDER[i]
        first = sub * SUB
        count = SUB - 1 if sub == SUBS - 1 else SUB
        await_bytes(got.at[g, pl.ds(first, count)], z_recv.at[g, sub])
        held = got[g, first:first + SUB].astype(F32)
        rows = jnp.concatenate([held[:, :CAP].reshape(PLACES, D // 2), held[:, CAP:].reshape(PLACES, D // 2)], axis=1)
        rows_of(i, sub, A0)[...] = rows.astype(BF16)
        for j in range(3):
            passed(i, sub, j).start()

    def pass_twin(i, sub):
        passed(i, sub, 0).wait_recv()
        passed(i, sub, 3).start()

    def learn_ranks():
        for copy in shared[:3]:
            copy.wait_recv()
        shared[3].start()
        for i, g in enumerate(ORDER):
            for s, a in enumerate(KEYS):
                rank = ranks[a, g]
                rank = jnp.where(rank > 0.5, rank, NEVER)
                keyed[i, s] = jnp.transpose(jnp.broadcast_to(rank, (BIG, BIG)))
        shared[3].wait_recv()
        for i in range(3):
            for j, a in enumerate(QUERIES):
                query[4 * i + j] = ranks[a, ORDER[i]]
        low = iota((1, BIG), 1) < SMALL
        for s, (a, b) in enumerate(((A1, A0), (R0, R1))):
            one, two = ranks[a, ORDER[3]], ranks[b, ORDER[3]]
            query[12 + s] = jnp.where(low, one, pltpu.roll(two, SMALL, 1))
            query[14 + s] = jnp.where(low, pltpu.roll(one, SMALL, 1), two)

    def dots(k, q):
        return lax.dot_general(k, q, (((1,), (1,)), ((), ())), preferred_element_type=F32)

    def rows_in(p, a, b):
        if p >= 3:
            return small[p - 3, a:b].reshape((b - a) * SMALL, D)
        return big[p, a:b].reshape((b - a) * BIG, D)

    def key_ranks(p, s):
        if p >= 3:
            return keyed[3, s, (p - 3) * SMALL:(p - 2) * SMALL]
        return keyed[p, s]

    def groups(q, far):
        if q >= 3:
            return [12 + 2 * (q - 3) + far]
        return [4 * q + 2 * far, 4 * q + 2 * far + 1]

    def fold(sims, rank, j):
        masked = jnp.where(rank < query[j], sims, -1.0)
        best[j] = jnp.maximum(best[j], jnp.max(masked.reshape(sims.shape[0] // 8, 8, 128), axis=0))

    def inner(k, q):
        sims = dots(rows_in(k, A0, R1), rows_in(q, A1, L0))
        size = sims.shape[0] // 3
        for s in range(3):
            for n, j in enumerate(groups(q, 0)):
                fold(sims[s * size:(s + 1) * size, n * 128:(n + 1) * 128], key_ranks(k, s), j)

    def own(k, q):
        sims = dots(rows_in(k, A0, L0), rows_in(q, A1, L0))
        for n, j in enumerate(groups(q, 0)):
            fold(sims[:, n * 128:(n + 1) * 128], key_ranks(k, 0), j)

    def beside(k, q):
        sims = dots(rows_in(k, L0, R1), rows_in(q, A1, L0))
        size = sims.shape[0] // 2
        for s in range(2):
            for n, j in enumerate(groups(q, 0)):
                fold(sims[s * size:(s + 1) * size, n * 128:(n + 1) * 128], key_ranks(k, 1 + s), j)

    def outer(k, q):
        sims = dots(rows_in(k, L0, R0), rows_in(q, R0, R1 + 1))
        for n, j in enumerate(groups(q, 1)):
            fold(sims[:, n * 128:(n + 1) * 128], key_ranks(k, 1), j)

    def pairs(p, work):
        for h in range(min(p, 3)):
            work(h, p)
            work(p, h)
        if p == 4:
            work(3, 4)
            work(4, 3)
        work(p, p)

    def subs_of(p):
        return [(p, sub) for sub in range(SUBS)] if p < 3 else [(3, 2 * (p - 3)), (3, 2 * (p - 3) + 1)]

    def compare_inner(p):
        for i, sub in subs_of(p):
            passed(i, sub, 2).wait_recv()
            passed(i, sub, 1).wait_recv()
        pairs(p, inner)

    def compare_outer(p):
        for i, sub in subs_of(p):
            passed(i, sub, 3).wait_recv()
        pairs(p, outer)

    for n in range(4 * SUBS):
        pass_on(n // SUBS, n % SUBS)
        if n + AHEAD < 4 * SUBS:
            along_z(n + AHEAD)
        if n == 1:
            gather_ranks()
        if n == SUBS:
            learn_ranks()
        if n >= LAG:
            pass_twin((n - LAG) // SUBS, (n - LAG) % SUBS)
        i, sub = divmod(n - LAG, SUBS)
        if sub == SUBS - 1 and 0 <= i < 3:
            compare_inner(i)
        if sub == 0 and 0 < i < 4:
            compare_outer(i - 1)
    compare_inner(3)
    compare_outer(3)
    pass_twin(3, 2)
    for i, sub in subs_of(4):
        passed(i, sub, 2).wait_recv()
    pairs(4, own)
    pass_twin(3, 3)
    for i, sub in subs_of(4):
        passed(i, sub, 1).wait_recv()
    pairs(4, beside)

    low = iota((1, BIG), 1) < SMALL

    def gather_top(one_set):
        for j in (2 * one_set, 2 * one_set + 1):
            a = QUERIES[j]
            for i in range(3):
                part[a, ORDER[i]] = jnp.max(best[4 * i + j], axis=0, keepdims=True)
            one, two = [jnp.max(best[m + one_set], axis=0, keepdims=True) for m in (12, 14)]
            part[a, ORDER[3]] = (jnp.where(low, one, pltpu.roll(two, SMALL, 1)) if a in (A1, R0) else
                                 jnp.where(low, pltpu.roll(one, SMALL, 1), two))

    halves = [remote(part.at[a], half.at[i], h_send.at[i], h_recv.at[i], twin) for i, a in enumerate((R1, A1))]
    gather_top(0)
    halves[1].start()
    compare_outer(4)
    gather_top(1)
    halves[0].start()
    for n, (a, dx) in enumerate(((R0, 1), (A0, 0))):
        halves[n].wait_recv()
        for g in (2, 1, 3, 0):
            whole[n, g] = jnp.maximum(part[a, g], half[n, g])
            if dx or g:
                remote(whole.at[n, g], other.at[n, g], p_send, p_recv.at[n], at(dx, NY - g, False, 0)).start()
    other[1, 0] = whole[1, 0]
    await_bytes(other.at[0], p_recv.at[0])
    await_bytes(other.at[1, pl.ds(1, 3)], p_recv.at[1])
    most = [jnp.maximum(other[0, g], other[1, g]) for g in range(NY)]
    for q, row in enumerate(turn(most)):
        turned[q] = row

    for b in reversed(range(NZ - 1)):
        remote(turned.at[b // SUB], back.at[b], b_send, b_recv, at(0, 0, False, NZ - WAY[b])).start()
    back[NZ - 1] = turned[SUBS - 1]

    for g in ORDER[1:]:
        along_y[g].wait_send()
    for copy in shared:
        copy.wait_send()
    await_bytes(rank_mid.at[pl.ds(1, NY - 1)], yr_send)
    await_bytes(rank_got.at[pl.ds(0, NZ - 1)], zr_send)
    await_bytes(got.at[:, pl.ds(0, NZ - 1)], z_send)
    for j in range(4):
        await_bytes(got, x_send.at[j])
    for copy in halves:
        copy.wait_send()
    await_bytes(back.at[pl.ds(0, 7)], p_send)

    await_bytes(back.at[pl.ds(0, NZ - 1)], b_recv)
    total = jnp.zeros((1, ROWS), F32)
    for g, held in enumerate(collect(back)):
        one = held.astype(BF16).astype(F32)
        two = (held - one).astype(BF16).astype(F32)
        three = held - one - two
        row = iota((16, BIG), 0)
        split = jnp.where(row == 0, one, jnp.where(row == 1, two, jnp.where(row == 2, three, 0.0))).astype(BF16)
        picked = jnp.dot(split, place[g * BIG:(g + 1) * BIG, :], preferred_element_type=F32)
        total = total + (picked[0:1] + picked[1:2] + picked[2:3])
    out_ref[...] = total.reshape(ROWS)
    await_bytes(back.at[pl.ds(0, NZ - 1)], b_send)


def local(embeddings, cluster_ids, order_keys):
    dma = pltpu.SemaphoreType.DMA
    vmem = pltpu.VMEM
    out = pl.pallas_call(
        kernel,
        out_shape=jax.ShapeDtypeStruct((ROWS,), F32),
        in_specs=[pl.BlockSpec(memory_space=pl.ANY)] * 3,
        out_specs=pl.BlockSpec(memory_space=vmem),
        scratch_shapes=[
            vmem((ROWS, D), BF16),
            vmem((1, ROWS), jnp.int32),
            vmem((1, ROWS), jnp.int32),
            vmem((NY * BIG, ROWS), BF16),
            vmem((NY, NZ, 16, D // 2), BF16),
            vmem((NY, NZ, 16, D // 2), BF16),
            vmem((NY, NZ, 16, D // 2), BF16),
            vmem((NY, 1, BIG), F32),
            vmem((NY, 1, BIG), F32),
            vmem((SUBS, 1, BIG), F32),
            vmem((NZ, 1, BIG), F32),
            vmem((5, NY, 1, BIG), F32),
            vmem((3, 5, BIG, D), BF16),
            vmem((2, 5, SMALL, D), BF16),
            vmem((4, 3, BIG, BIG), F32),
            vmem((16, 1, BIG), F32),
            vmem((16, 8, BIG), F32),
            vmem((5, NY, 1, BIG), F32),
            vmem((2, NY, 1, BIG), F32),
            vmem((2, NY, 1, BIG), F32),
            vmem((2, NY, 1, BIG), F32),
            vmem((SUBS, 1, BIG), F32),
            vmem((NZ, 1, BIG), F32),
            dma((3,)), pltpu.SemaphoreType.REGULAR((2, NZ // 2 + 1)), dma((NY,)), dma((NY,)), dma, dma, dma, dma((NY, SUBS)), dma, dma,
            dma((4,)), dma((4 * SUBS, 4)), dma((4,)), dma((4,)), dma((2,)), dma((2,)), dma, dma((2,)), dma, dma,
        ],
        compiler_params=pltpu.CompilerParams(collective_id=0, has_side_effects=True, vmem_limit_bytes=56 * 2**20),
    )(embeddings, cluster_ids.reshape(1, ROWS), order_keys.reshape(1, ROWS))
    return out


def solution(mesh):
    placed = (P(("shard", "slot"), None), P(("shard", "slot")), P(("shard", "slot")))
    return jax.shard_map(local, mesh=mesh, in_specs=placed, out_specs=P(("shard", "slot")), check_vma=False)
```
